512 devices in a mesh: gx: 8 (over z_lo), gy: 16 (over z_hi, x, core), gz: 4 (over y).
Axes of the slice: x: 4, y: 4, z: 16 (z_hi: 2, z_lo: 8; z = z_hi * 8 + z_lo), core: 2. Of those that a mesh axis runs over, the one named last changes fastest.
Arguments:
- voltage_gradient_components: float32 [3, 128, 128, 1024], P(None, 'gx', 'gy', 'gz'), may hold values from -6 to 6
- flux_curl_components: float32 [3, 128, 128, 1024], P(None, 'gx', 'gy', 'gz'), may hold values from -6 to 6
- phase_label_grid: int32 [128, 128, 1024], P('gx', 'gy', 'gz'), may hold values from 0 to 3
- feeding_spot_positions: int32 [512, 16], P(('gx', 'gy', 'gz')), may hold values from 0 to 32767
- thermal_rise_kelvin: float32 [64, 64, 512], P('gx', ('gy', 'gz')), may hold values from 0 to 1
- packing_fraction: float32 [64, 64, 512], P('gx', ('gy', 'gz')), may hold values from 0.55 to 0.95
Outputs:
- temp_out: float32 [64, 64, 512], P('gx', ('gy', 'gz'))
- density_out: float32 [64, 64, 512], P('gx', ('gy', 'gz'))
The draws below stay inside these ranges and needn't reach their ends.
Inputs may be any that keep to these rules, and one draw needn't show every extreme that they name: `feeding_spot_positions`: each entry is a cell index inside its own brick, x-major; several may name the same cell.
All inputs are finite; a program needn't handle non-finite values.
Results may differ from the reference program's by a relative error of at most 0.0001.
Values sent between devices are 32-bit elements; how exact they have to be, the bound alone decides.
No kernel may reach another device: no remote copies, remote signals or barrier semaphores. Data moves between devices by JAX's collectives and lax.ppermute only.
A program may use at most 64 MiB of HBM per device.

```python
import math
import jax
import jax.numpy as jnp

CX = 16
CY = 8
CZ = 256
ITERS = 4
HEAT_STEPS = 2
SRC_DEV = 16
MESH_SPAN_WIDTH = 128
MESH_SPAN_BREADTH = 128
MESH_SPAN_HEIGHT = 1024
BRICKS = 512
N_GX = 8
N_GY = 16
N_GZ = 4


def place_ends(values, stream_key, low, largest):
    dims = values.shape
    place = [jax.random.randint(jax.random.fold_in(stream_key, axis), (), 0, dims[axis]) for axis in range(len(dims))]
    values = values.at[tuple(place)].set(low)
    longest = dims.index(max(dims))
    place[longest] = (place[longest] + 1) % dims[longest]
    return values.at[tuple(place)].set(largest)


def shard_levels(key, shape, split, smallest, high):
    loudness = 1.0
    for dim, blocks in split:
        steps = jax.random.uniform(jax.random.fold_in(jax.random.fold_in(key, 6), dim), (blocks,), jnp.float32, smallest / len(split), high / len(split))
        loudness = loudness * jnp.repeat(jnp.exp(steps), shape[dim] // blocks).reshape((-1,) + (1,) * (len(shape) - 1 - dim))
    return loudness


def centred(key, shape, spread, bound, split=(), held_as=jnp.bfloat16):
    entries = jax.random.normal(key, shape, jnp.float32) * spread
    if len(split) > 0:
        entries = shard_levels(key, shape, split, -0.22, 0.18) * entries
    return jnp.clip(entries, min=-bound, max=bound).astype(held_as)


def setup_inputs(seed: int = 0) -> dict:
    keys = jax.random.split(jax.random.key(seed), 7)
    return {
        "voltage_gradient_components": centred(keys[0], (3, MESH_SPAN_WIDTH, MESH_SPAN_BREADTH, MESH_SPAN_HEIGHT), 1.0, 6.0, ((1, 8), (2, 16), (3, 4)), jnp.float32),
        "flux_curl_components": centred(keys[1], (3, MESH_SPAN_WIDTH, MESH_SPAN_BREADTH, MESH_SPAN_HEIGHT), 1.0, 6.0, ((1, 8), (2, 16), (3, 4)), jnp.float32),
        "phase_label_grid": place_ends(jax.random.randint(keys[2], (MESH_SPAN_WIDTH, MESH_SPAN_BREADTH, MESH_SPAN_HEIGHT), 0, 4), jax.random.fold_in(keys[2], 1), 0, 3).astype(jnp.int32),
        "feeding_spot_positions": place_ends(jax.random.randint(keys[3], (BRICKS, SRC_DEV), 0, CX * CY * CZ), jax.random.fold_in(keys[3], 1), 0, (CX * CY * CZ) - 1).astype(jnp.int32),
        "thermal_rise_kelvin": jnp.clip(1.0 * jax.random.uniform(keys[4], (MESH_SPAN_WIDTH // 2, MESH_SPAN_BREADTH // 2, MESH_SPAN_HEIGHT // 2), jnp.float32) ** shard_levels(keys[4], (MESH_SPAN_WIDTH // 2, MESH_SPAN_BREADTH // 2, MESH_SPAN_HEIGHT // 2), ((0, 8), (1, 64)), -0.2, 0.2), 0.0, 1.0),
        "packing_fraction": jnp.clip(0.55 + 0.39999998 * jax.random.uniform(keys[5], (MESH_SPAN_WIDTH // 2, MESH_SPAN_BREADTH // 2, MESH_SPAN_HEIGHT // 2), jnp.float32) ** shard_levels(keys[5], (MESH_SPAN_WIDTH // 2, MESH_SPAN_BREADTH // 2, MESH_SPAN_HEIGHT // 2), ((0, 8), (1, 64)), -0.2, 0.2), 0.55, 0.95),
    }


eps_table = (3.0, 9.0, 12.0, 1.0)
sig_table = (0.05, 0.01, 0.4, 0.0)
courant_dt = 0.99 / math.sqrt(3.0)

def lookup(phase_label_grid, table):
    result = jnp.zeros(phase_label_grid.shape, jnp.float32)
    for index in range(4):
        result = result + (phase_label_grid == index).astype(jnp.float32) * table[index]
    return result

def ahead(field, axis):
    size = field.shape[axis]
    inner = jax.lax.slice_in_dim(field, 1, size, axis=axis)
    zeros_plane = jnp.zeros_like(jax.lax.slice_in_dim(field, 0, 1, axis=axis))
    return jnp.concatenate([inner, zeros_plane], axis=axis)

def behind(field, axis):
    size = field.shape[axis]
    inner = jax.lax.slice_in_dim(field, 0, size - 1, axis=axis)
    zeros_plane = jnp.zeros_like(jax.lax.slice_in_dim(field, 0, 1, axis=axis))
    return jnp.concatenate([zeros_plane, inner], axis=axis)

def reference(voltage_gradient_components, flux_curl_components, phase_label_grid, feeding_spot_positions, thermal_rise_kelvin, packing_fraction):
    eps_map = lookup(phase_label_grid, eps_table)
    sig_map = lookup(phase_label_grid, sig_table)
    loss = sig_map * courant_dt / (2.0 * eps_map)
    coef_a = (1.0 - loss) / (1.0 + loss)
    coef_b = courant_dt / (eps_map * (1.0 + loss))
    brick = jnp.arange(N_GX * N_GY * N_GZ, dtype=jnp.int32)[:, None]
    brick_x = brick // (N_GY * N_GZ)
    brick_y = brick // N_GZ % N_GY
    brick_z = brick % N_GZ
    cell_x = brick_x * CX + feeding_spot_positions // (CY * CZ)
    cell_y = brick_y * CY + feeding_spot_positions // CZ % CY
    cell_z = brick_z * CZ + feeding_spot_positions % CZ
    flat = ((cell_x * MESH_SPAN_BREADTH + cell_y) * MESH_SPAN_HEIGHT + cell_z).reshape(-1).astype(jnp.int32)
    count = jnp.zeros((MESH_SPAN_WIDTH * MESH_SPAN_BREADTH * MESH_SPAN_HEIGHT,), jnp.float32).at[flat].add(1.0).reshape(MESH_SPAN_WIDTH, MESH_SPAN_BREADTH, MESH_SPAN_HEIGHT)
    efield_first, efield_second, efield_third = (voltage_gradient_components[0], voltage_gradient_components[1], voltage_gradient_components[2])
    hfield_first, hfield_second, hfield_third = (flux_curl_components[0], flux_curl_components[1], flux_curl_components[2])
    deposited_microwave_joules = jnp.zeros((MESH_SPAN_WIDTH // 2, MESH_SPAN_BREADTH // 2, MESH_SPAN_HEIGHT // 2), jnp.float32)
    for step in range(ITERS):
        hfield_first = hfield_first - courant_dt * (ahead(efield_third, 1) - efield_third - (ahead(efield_second, 2) - efield_second))
        hfield_second = hfield_second - courant_dt * (ahead(efield_first, 2) - efield_first - (ahead(efield_third, 0) - efield_third))
        hfield_third = hfield_third - courant_dt * (ahead(efield_second, 0) - efield_second - (ahead(efield_first, 1) - efield_first))
        wave = 60.0 * math.sin(0.6 * (step + 0.5) * courant_dt)
        efield_first = coef_a * efield_first + coef_b * (hfield_third - behind(hfield_third, 1) - (hfield_second - behind(hfield_second, 2)))
        efield_second = coef_a * efield_second + coef_b * (hfield_first - behind(hfield_first, 2) - (hfield_third - behind(hfield_third, 0)))
        efield_third = coef_a * efield_third + coef_b * (hfield_second - behind(hfield_second, 0) - (hfield_first - behind(hfield_first, 1))) - coef_b * count * wave
        power = sig_map * (efield_first * efield_first + efield_second * efield_second + efield_third * efield_third)
        deposited_microwave_joules = deposited_microwave_joules + power.reshape(MESH_SPAN_WIDTH // 2, 2, MESH_SPAN_BREADTH // 2, 2, MESH_SPAN_HEIGHT // 2, 2).mean(axis=(1, 3, 5))
    deposited_microwave_joules = deposited_microwave_joules / ITERS
    for step in range(HEAT_STEPS):
        bordered_warmth = jnp.pad(thermal_rise_kelvin, 1)
        spreading_stencil_matrix = bordered_warmth[2:, 1:-1, 1:-1] + bordered_warmth[:-2, 1:-1, 1:-1] + bordered_warmth[1:-1, 2:, 1:-1] + bordered_warmth[1:-1, :-2, 1:-1] + bordered_warmth[1:-1, 1:-1, 2:] + bordered_warmth[1:-1, 1:-1, :-2] - 6.0 * thermal_rise_kelvin
        advanced_thermal_rise = thermal_rise_kelvin + 0.1 * ((0.2 + packing_fraction) * spreading_stencil_matrix + 10.0 * deposited_microwave_joules)
        packing_fraction = packing_fraction + 0.3 * (1.0 - packing_fraction) * jnp.exp(-3.0 / (1.0 + thermal_rise_kelvin))
        thermal_rise_kelvin = advanced_thermal_rise
    return (thermal_rise_kelvin, packing_fraction)
```

```python
import functools
import math

import jax
import jax.numpy as jnp
from jax import lax
from jax.experimental import pallas as pl
from jax.experimental.pallas import tpu as pltpu
from jax.sharding import PartitionSpec as P

ITERS = 4
W = 4
CX, CY, CZ = 16, 8, 256
NX, NY = CX + 2 * W, CY + 2 * W
LANES = 128
FIELDS = 8
TILES = 2 * FIELDS

eps_table = (3.0, 9.0, 12.0, 1.0)
sig_table = (0.05, 0.01, 0.4, 0.0)
courant_dt = 0.99 / math.sqrt(3.0)
loss_table = tuple(s * courant_dt / (2.0 * e) for s, e in zip(sig_table, eps_table))
ca_table = tuple((1.0 - l) / (1.0 + l) for l in loss_table)
cb_table = tuple(courant_dt / (e * (1.0 + l)) for l, e in zip(loss_table, eps_table))

F32 = jnp.float32
VMEM = pl.BlockSpec(memory_space=pltpu.VMEM)
SMEM = pl.BlockSpec(memory_space=pltpu.SMEM)
PARAMS = pltpu.CompilerParams(vmem_limit_bytes=48 * 1024 * 1024)


def f32(*shape):
    return jax.ShapeDtypeStruct(shape, F32)


def call(body, outs, ins, scratch=(), flops=0, size=0):
    return pl.pallas_call(
        body,
        out_shape=outs,
        in_specs=ins,
        out_specs=jax.tree.map(lambda _: VMEM, outs),
        scratch_shapes=list(scratch),
        compiler_params=PARAMS,
        cost_estimate=pl.CostEstimate(flops=flops, bytes_accessed=size, transcendentals=0),
    )


def swaps(size, first):
    pairs = [(i, i + 1) for i in range(first, size - 1, 2)]
    return pairs + [(j, i) for i, j in pairs]


def shifts(size, step):
    return [(i, i + step) for i in range(size) if 0 <= i + step < size]


def lane_ids(shape):
    return lax.broadcasted_iota(jnp.int32, shape, len(shape) - 1)


def pack_kernel(place, spots, e_ref, h_ref, phase_ref, own, out_a, out_b, z_up, z_down):
    odd = place[0]
    for y in range(CY):
        for t in range(2):
            rows = pl.ds(t * CY + y, CX, stride=2 * CY)
            for c in range(3):
                own[2 * c + t, y] = e_ref[c, rows, :]
                own[2 * (c + 3) + t, y] = h_ref[c, rows, :]
            own[12 + t, y] = (phase_ref[rows, :] + 1).astype(F32)
            own[14 + t, y] = jnp.zeros((CX, LANES), F32)

    lane = lane_ids((1, LANES))

    def drop(i, carry):
        spot = spots[0, i]
        x, y = spot >> 11, (spot >> 8) & (CY - 1)
        t, place_z = 14 + ((spot >> 7) & 1), spot & (LANES - 1)
        row = own[t, y, pl.ds(x, 1), :]
        own[t, y, pl.ds(x, 1), :] = row + (lane == place_z).astype(F32)
        return carry

    lax.fori_loop(0, spots.shape[1], drop, 0)

    wide = lane_ids((CX, LANES))
    slot = wide // 8
    upper = wide % 8 >= W
    for y in range(CY):
        up = jnp.zeros((CX, LANES), F32)
        down = jnp.zeros((CX, LANES), F32)
        for f in range(FIELDS):
            here = slot == f
            up = jnp.where(here & ~upper, pltpu.roll(own[2 * f + 1, y], 8 * f + W, 1), up)
            down = jnp.where(here & upper, pltpu.roll(own[2 * f, y], 8 * f + W, 1), down)
        z_up[y] = up
        z_down[y] = down
    start_a = odd * (CY - W)
    start_b = (1 - odd) * (CY - W)
    for k in range(TILES):
        for i in range(W):
            out_a[k, i] = own[k, start_a + i]
            out_b[k, i] = own[k, start_b + i]


def edge_kernel(place, z_up, z_down, own_z, out_a, out_b):
    odd = place[0]
    own_z[...] = z_up[...] + z_down[...]
    start_a = odd * (CY - W)
    start_b = (1 - odd) * (CY - W)
    for i in range(W):
        out_a[i] = own_z[start_a + i]
        out_b[i] = own_z[start_b + i]


def side_kernel(place, own, own_z, in_a, in_b, z_a, z_b, out_up, out_down):
    odd = place[0]
    block_a, block_b = 3 * odd, 3 * (1 - odd)

    def move(read, k, block, first):
        for i in range(W):
            rows = read(first + i)
            out_up[k, block, pl.ds(W * i, W), :] = rows[CX - W :]
            out_down[k, block, pl.ds(W * i, W), :] = rows[:W]

    for k in range(TILES):
        for b in range(CY // W):
            move(lambda i: own[k, i], k, 1 + b, W * b)
        move(lambda i: in_a[k, i], k, block_a, 0)
        move(lambda i: in_b[k, i], k, block_b, 0)
    for b in range(CY // W):
        move(lambda i: own_z[i], TILES, 1 + b, W * b)
    move(lambda i: z_a[i], TILES, block_a, 0)
    move(lambda i: z_b[i], TILES, block_b, 0)


def field_kernel(place, own, own_z, in_a, in_b, z_a, z_b, from_low, from_high, out, s, zs, coef, power, pair):
    odd = place[0]
    first_a, first_b = odd * (CY + W), (1 - odd) * (CY + W)
    wide = lane_ids((NX, LANES))
    near = (wide < W) | (wide >= LANES - W)

    def settle(j, block, i, read, read_z):
        for k in range(TILES + 1):
            rows = jnp.concatenate(
                [
                    from_low[k, block, pl.ds(W * i, W), :],
                    read_z() if k == TILES else read(k),
                    from_high[k, block, pl.ds(W * i, W), :],
                ],
                axis=0,
            )
            if k == TILES:
                for f in range(FIELDS):
                    turned = pltpu.roll(rows, LANES - (8 * f + W), 1)
                    s[f, j, :, 2 * LANES :] = jnp.where(near, turned, 0.0)
            else:
                s[k // 2, j, :, pl.ds((k % 2) * LANES, LANES)] = rows

    for i in range(W):
        for b in range(CY // W):
            y = W * b + i
            settle(W + y, 1 + b, i, lambda k: own[k, y], lambda: own_z[y])
        settle(first_a + i, 3 * odd, i, lambda k: in_a[k, i], lambda: z_a[i])
        settle(first_b + i, 3 * (1 - odd), i, lambda k: in_b[k, i], lambda: z_b[i])

    def coefs(j, carry):
        phase = s[6, j]

        def chosen(table):
            value = jnp.zeros_like(phase)
            for index in range(4):
                value = jnp.where(phase == index + 1.0, table[index], value)
            return value

        coef[0, j] = chosen(ca_table)
        coef[1, j] = chosen(cb_table)
        coef[2, j] = chosen(sig_table)
        coef[3, j] = jnp.where(phase > 0.0, courant_dt, 0.0)
        power[j] = jnp.zeros_like(phase)
        return carry

    lax.fori_loop(0, NY, coefs, 0)

    span = 3 * LANES
    for step in range(ITERS):
        wave = 60.0 * math.sin(0.6 * (step + 0.5) * courant_dt)

        def plane(j, carry):
            back = jnp.maximum(j - 1, 0)
            ex, ey, ez = s[0, j], s[1, j], s[2, j]
            step_h = coef[3, j]
            hx = s[3, j] - step_h * ((s[2, j + 1] - ez) - (pltpu.roll(ey, span - 1, 1) - ey))
            hy = s[4, j] - step_h * ((pltpu.roll(ex, span - 1, 1) - ex) - (pltpu.roll(ez, NX - 1, 0) - ez))
            hz = s[5, j] - step_h * ((pltpu.roll(ey, NX - 1, 0) - ey) - (s[0, j + 1] - ex))
            s[3, j] = hx
            s[4, j] = hy
            s[5, j] = hz
            ca, cb, sig = coef[0, j], coef[1, j], coef[2, j]
            ex = ca * ex + cb * ((hz - s[5, back]) - (hy - pltpu.roll(hy, 1, 1)))
            ey = ca * ey + cb * ((hx - pltpu.roll(hx, 1, 1)) - (hz - pltpu.roll(hz, 1, 0)))
            ez = ca * ez + cb * ((hy - pltpu.roll(hy, 1, 0)) - (hx - s[3, back])) - cb * s[7, j] * wave
            s[0, j] = ex
            s[1, j] = ey
            s[2, j] = ez
            power[j] += sig * (ex * ex + ey * ey + ez * ez)
            return carry

        lax.fori_loop(step, NY - 1 - step, plane, 0)

    rows = []
    for t in range(CY // 2):
        halves = []
        for k in range(2):
            lanes = pl.ds(k * LANES, LANES)
            pair[...] = power[W + 2 * t, :, lanes] + power[W + 2 * t + 1, :, lanes]
            halves.append(pair[pl.ds(W, CX // 2, stride=2), :] + pair[pl.ds(W + 1, CX // 2, stride=2), :])
        rows.append(jnp.concatenate(halves, axis=1))
    stacked = jnp.concatenate(rows, axis=0)
    source = lax.broadcasted_iota(jnp.int32, (2 * LANES, LANES), 0)
    target = lax.broadcasted_iota(jnp.int32, (2 * LANES, LANES), 1)
    gather = (source // 2 == target).astype(F32)
    summed = jnp.dot(stacked, gather, precision=lax.Precision.HIGHEST, preferred_element_type=F32)
    out[...] = (summed * (1.0 / (8.0 * ITERS))).reshape(CY // 2, CX // 2, LANES)


def laplacian(t, side_a, side_b, before, after):
    rows, span = t.shape
    wide = lane_ids((rows, span))
    x = lax.broadcasted_iota(jnp.int32, (rows, span), 0)
    up_x = jnp.where(x == rows - 1, after, pltpu.roll(t, rows - 1, 0))
    down_x = jnp.where(x == 0, before, pltpu.roll(t, 1, 0))
    up_z = jnp.where(wide == span - 1, 0.0, pltpu.roll(t, span - 1, 1))
    down_z = jnp.where(wide == 0, 0.0, pltpu.roll(t, 1, 1))
    return up_x + down_x + side_a + side_b + up_z + down_z - 6.0 * t


def densified(packing, warmth):
    return packing + 0.3 * (1.0 - packing) * jnp.exp(-3.0 / (1.0 + warmth))


def warm_kernel(t_ref, p_ref, side_a, side_b, before, after, base, packed):
    t, p = t_ref[...], p_ref[...]
    lap = laplacian(t, side_a[...], side_b[...], before[...], after[...])
    base[...] = t + 0.1 * ((0.2 + p) * lap)
    packed[...] = densified(p, t)


def first_kernel(base, packed, heat, warmth, density):
    for k in range(heat.shape[0]):
        lanes = pl.ds(k * LANES, LANES)
        t = base[:, lanes] + heat[k]
        warmth[:, lanes] = t
        density[:, lanes] = densified(packed[:, lanes], t)


def second_kernel(t_ref, p_ref, heat, side_a, side_b, before, after, warmth):
    t = t_ref[...]
    lap = laplacian(t, side_a[...], side_b[...], before[...], after[...])
    grown = t + 0.1 * ((0.2 + p_ref[...]) * lap)
    for k in range(heat.shape[0]):
        lanes = slice(k * LANES, (k + 1) * LANES)
        warmth[:, lanes] = grown[:, lanes] + heat[k]


def around(t):
    pencils = lax.axis_size("gy") * lax.axis_size("gz")
    side_a = lax.ppermute(t, ("gy", "gz"), swaps(pencils, 1))
    side_b = lax.ppermute(t, ("gy", "gz"), swaps(pencils, 0))
    bricks = lax.axis_size("gx")
    before = lax.ppermute(t[-1:], "gx", shifts(bricks, 1))
    after = lax.ppermute(t[:1], "gx", shifts(bricks, -1))
    return side_a, side_b, before, after


def tile_rows(a):
    lead = a.shape[:-3]
    a = a.reshape(lead + (CX, CY, 2, LANES))
    return jnp.swapaxes(a, -3, -2).reshape(lead + (2 * CX * CY, LANES))


def local(e, h, phase, spots, warmth, packing):
    n_y, n_z, n_x = lax.axis_size("gy"), lax.axis_size("gz"), lax.axis_size("gx")
    place = (lax.axis_index("gy") % 2).astype(jnp.int32).reshape(1)
    across, within = swaps(n_y, 1), swaps(n_y, 0)
    warmth = warmth.reshape(CX // 2, -1)
    packing = packing.reshape(CX // 2, -1)
    pencil = f32(*warmth.shape)

    own, to_a, to_b, z_up, z_down = call(
        pack_kernel,
        (f32(TILES, CY, CX, LANES), f32(TILES, W, CX, LANES), f32(TILES, W, CX, LANES), f32(CY, CX, LANES), f32(CY, CX, LANES)),
        [SMEM, SMEM, VMEM, VMEM, VMEM],
    )(place, spots, tile_rows(e), tile_rows(h), tile_rows(phase))
    in_a = lax.ppermute(to_a, "gy", across)
    in_b = lax.ppermute(to_b, "gy", within)
    z_up = lax.ppermute(z_up, "gz", shifts(n_z, 1))
    z_down = lax.ppermute(z_down, "gz", shifts(n_z, -1))
    own_z, z_a, z_b = call(
        edge_kernel,
        (f32(CY, CX, LANES), f32(W, CX, LANES), f32(W, CX, LANES)),
        [SMEM, VMEM, VMEM],
    )(place, z_up, z_down)
    z_a = lax.ppermute(z_a, "gy", across)
    z_b = lax.ppermute(z_b, "gy", within)

    base, packed = call(warm_kernel, (pencil, pencil), [VMEM] * 6)(warmth, packing, *around(warmth))

    block = f32(TILES + 1, NY // W, W * W, LANES)
    to_up, to_down = call(side_kernel, (block, block), [SMEM] + [VMEM] * 6)(
        place, own, own_z, in_a, in_b, z_a, z_b
    )
    from_low = lax.ppermute(to_up, "gx", shifts(n_x, 1))
    from_high = lax.ppermute(to_down, "gx", shifts(n_x, -1))
    heat = call(
        field_kernel,
        f32(CY // 2, CX // 2, LANES),
        [SMEM] + [VMEM] * 8,
        scratch=[
            pltpu.VMEM((FIELDS, NY, NX, 3 * LANES), F32),
            pltpu.VMEM((NX, LANES), F32),
            pltpu.VMEM((4, NY, NX, 3 * LANES), F32),
            pltpu.VMEM((NY, NX, 3 * LANES), F32),
            pltpu.VMEM((NX, LANES), F32),
        ],
    )(place, own, own_z, in_a, in_b, z_a, z_b, from_low, from_high)
    heat = lax.all_to_all(heat, "gz", split_axis=0, concat_axis=0, tiled=True)
    warmth, density = call(first_kernel, (pencil, pencil), [VMEM] * 3)(base, packed, heat)
    result = call(second_kernel, pencil, [VMEM] * 7)(warmth, packed, heat, *around(warmth))
    shape = (CX // 2, 1, -1)
    return result.reshape(shape), density.reshape(shape)


def solution(mesh):
    return jax.shard_map(
        local,
        mesh=mesh,
        in_specs=(
            P(None, "gx", "gy", "gz"),
            P(None, "gx", "gy", "gz"),
            P("gx", "gy", "gz"),
            P(("gx", "gy", "gz"), None),
            P("gx", ("gy", "gz"), None),
            P("gx", ("gy", "gz"), None),
        ),
        out_specs=(P("gx", ("gy", "gz"), None), P("gx", ("gy", "gz"), None)),
        check_vma=False,
    )
```

```python
import math

import jax
import jax.numpy as jnp
from jax import lax
from jax.experimental import pallas as pl
from jax.experimental.pallas import tpu as pltpu
from jax.sharding import PartitionSpec as P

ITERS = 4
W = 4
CX, CY, CZ = 16, 8, 256
TX, TY = CX // 2, CY // 2
PAD = W
NX, NY = CX + 2 * PAD, CY + 2 * W
LANES = 128
FIELDS = 8
TILES = 2 * FIELDS

eps_table = (3.0, 9.0, 12.0, 1.0)
sig_table = (0.05, 0.01, 0.4, 0.0)
courant_dt = 0.99 / math.sqrt(3.0)
loss_table = tuple(s * courant_dt / (2.0 * e) for s, e in zip(sig_table, eps_table))
ca_table = tuple((1.0 - l) / (1.0 + l) for l in loss_table)
cb_table = tuple(courant_dt / (e * (1.0 + l)) for l, e in zip(loss_table, eps_table))

F32 = jnp.float32
VMEM = pl.BlockSpec(memory_space=pltpu.VMEM)
HBM = pl.BlockSpec(memory_space=pltpu.HBM)

Y_PLANES = (4, 4, 4, 4, 3, 4, 3, 3)
Y_START = []
for planes in Y_PLANES:
    Y_START += [sum(2 * p for p in Y_PLANES[: len(Y_START) // 2]), 0]
    Y_START[-1] = Y_START[-2] + planes
Y_TOTAL = 2 * sum(Y_PLANES)


def side_rows(low):
    table, place = {}, 0
    for k in range(TILES + 1):
        field = k // 2
        most = W - 1 if field in ((3, 6, 7) if low else (3, 4, 5, 6, 7)) else W
        for j in range(NY):
            corner = W - j if low else j - (W + CY - 1)
            count = min(most, W - corner) if corner > 0 else most
            table[k, j] = (place, count)
            place += count
    return table, place


LOW_TABLE, LOW_ROWS = side_rows(True)
HIGH_TABLE, HIGH_ROWS = side_rows(False)


def f32(*shape):
    return jax.ShapeDtypeStruct(shape, F32)


def call(body, outs, ins, scratch=(), limit=24):
    return pl.pallas_call(
        body,
        out_shape=outs,
        in_specs=ins,
        out_specs=jax.tree.map(lambda _: VMEM, outs),
        scratch_shapes=list(scratch),
        compiler_params=pltpu.CompilerParams(vmem_limit_bytes=limit * 1024 * 1024),
    )


def swaps(size, first):
    pairs = [(i, i + 1) for i in range(first, size - 1, 2)]
    return pairs + [(j, i) for i, j in pairs]


def shifts(size, step):
    return [(i, i + step) for i in range(size) if 0 <= i + step < size]


def lane_ids(shape):
    return lax.broadcasted_iota(jnp.int32, shape, len(shape) - 1)


def parity():
    return lax.rem(lax.axis_index("gy"), 2)


def pack_kernel(spots_hbm, e_hbm, h_hbm, phase_hbm, t_hbm, own, out_a, out_b, shared, spots, e_ref, h_ref, phase_ref, heat, sems):
    odd = parity()
    copies = [
        pltpu.make_async_copy(spots_hbm, spots, sems.at[0]),
        pltpu.make_async_copy(phase_hbm, phase_ref, sems.at[1]),
    ]
    for c in range(3):
        copies.append(pltpu.make_async_copy(e_hbm.at[c], e_ref.at[c], sems.at[2 + c]))
    for c in range(3):
        copies.append(pltpu.make_async_copy(h_hbm.at[c], h_ref.at[c], sems.at[5 + c]))
    copies.append(pltpu.make_async_copy(t_hbm, heat, sems.at[8]))
    for copy in copies:
        copy.start()
    for t in range(2):
        own[14 + t] = jnp.zeros((CY, CX, LANES), F32)

    lane = lane_ids((1, LANES))

    def drop(i, carry):
        spot = spots[0, i]
        x, y = spot >> 11, (spot >> 8) & (CY - 1)
        t, place_z = 14 + ((spot >> 7) & 1), spot & (LANES - 1)
        row = own[t, y, pl.ds(x, 1), :]
        own[t, y, pl.ds(x, 1), :] = row + (lane == place_z).astype(F32)
        return carry

    copies[0].wait()
    lax.fori_loop(0, spots.shape[1], drop, 0)

    def spread(k, source):
        for y in range(CY):
            for t in range(2):
                own[k + t, y] = source[pl.ds(t * CY + y, CX, stride=2 * CY), :].astype(F32)

    copies[1].wait()
    phase_ref[...] += 1
    spread(12, phase_ref)
    for c in range(3):
        copies[2 + c].wait()
        spread(2 * c, e_ref.at[c])
    for c in range(3):
        copies[5 + c].wait()
        spread(2 * (3 + c), h_ref.at[c])
    for k in range(TILES):
        planes = Y_PLANES[k // 2]
        for i in range(planes):
            out_a[Y_START[k] + i] = own[k, odd * (CY - planes) + i]
            out_b[Y_START[k] + i] = own[k, (1 - odd) * (CY - planes) + i]

    wide = lane_ids((CX, LANES))
    slot = wide // 8
    upper = wide % 8 >= W
    for y in range(CY):
        edge = jnp.zeros((CX, LANES), F32)
        for f in range(FIELDS):
            shift = 8 * f + W
            ends = jnp.where(upper, pltpu.roll(own[2 * f, y], shift, 1), pltpu.roll(own[2 * f + 1, y], shift, 1))
            edge = jnp.where(slot == f, ends, edge)
        shared[pl.ds(CX * y, CX), :] = edge
    copies[8].wait()
    for k in range(heat.shape[2] // LANES):
        shared[pl.ds(CX * CY + k * TX, TX), :] = heat[:, 0, pl.ds(k * LANES, LANES)]


def edge_kernel(from_below, from_above, own_z, out_a, out_b):
    odd, me = parity(), lax.axis_index("gz")
    upper = lane_ids((CX, LANES)) % 8 >= W
    has_below = (me > 0).astype(F32)
    has_above = (me < lax.axis_size("gz") - 1).astype(F32)
    for y in range(CY):
        rows = pl.ds(CX * y, CX)
        own_z[y] = jnp.where(upper, from_above[rows, :] * has_above, from_below[rows, :] * has_below)
    thermal = pl.ds(CX * CY, from_below.shape[0] - CX * CY)
    below, above = from_below[thermal, :], from_above[thermal, :]
    for out, up in ((out_a, odd), (out_b, 1 - odd)):
        for i in range(W):
            out[pl.ds(CX * i, CX), :] = own_z[up * (CY - W) + i]
        out[pl.ds(CX * W, thermal.size), :] = jnp.where(up == 1, below, above)


def side_kernel(own, own_z, in_a, in_b, z_a, z_b, warmth, out_up, out_down):
    odd = parity()

    def move(k, j, read):
        for out, table, up in ((out_up, LOW_TABLE, True), (out_down, HIGH_TABLE, False)):
            start, count = table[k, j]
            if count:
                rows = read()
                out[pl.ds(start, count), :] = rows[CX - count :] if up else rows[:count]

    for y in range(CY):
        for k in range(TILES):
            move(k, W + y, lambda: own[k, y])
        move(TILES, W + y, lambda: own_z[y])
    for k in range(warmth.shape[0] // TX):
        out_up[pl.ds(LOW_ROWS + k, 1), :] = warmth[pl.ds(k * TX + TX - 1, 1), :]
        out_down[pl.ds(HIGH_ROWS + k, 1), :] = warmth[pl.ds(k * TX, 1), :]

    def outside(low, high, z_low, z_high):
        for k in range(TILES):
            planes = Y_PLANES[k // 2]
            for i in range(planes):
                move(k, W - planes + i, lambda: low[Y_START[k] + i])
                move(k, W + CY + i, lambda: high[Y_START[k] + i])
        for i in range(W):
            move(TILES, i, lambda: z_low[pl.ds(CX * i, CX), :])
            move(TILES, W + CY + i, lambda: z_high[pl.ds(CX * i, CX), :])
    @pl.when(odd == 1)
    def _():
        outside(in_b, in_a, z_b, z_a)

    @pl.when(odd == 0)
    def _():
        outside(in_a, in_b, z_a, z_b)


def field_kernel(own, own_z, in_a, in_b, z_a, z_b, from_low, from_high, out, s, zs, coef, reach, power, pair):
    odd = parity()
    span = 3 * LANES
    middle = pl.ds(PAD, CX)
    outer = (pl.ds(0, PAD), pl.ds(PAD + CX, PAD))

    def lanes(k):
        return pl.ds((k % 2) * LANES, LANES)

    blank = jnp.zeros((PAD, LANES), F32)
    for j in range(NY):
        for rows in outer:
            for k in range(TILES):
                s[k // 2, j, rows, lanes(k)] = blank
            zs[j, rows, :] = blank
        for k in range(TILES + 1):
            start, count = LOW_TABLE[k, j]
            if count:
                part = from_low[pl.ds(start, count), :]
                if k < TILES:
                    s[k // 2, j, pl.ds(PAD - count, count), lanes(k)] = part
                else:
                    zs[j, pl.ds(PAD - count, count), :] = part
            start, count = HIGH_TABLE[k, j]
            if count:
                part = from_high[pl.ds(start, count), :]
                if k < TILES:
                    s[k // 2, j, pl.ds(PAD + CX, count), lanes(k)] = part
                else:
                    zs[j, pl.ds(PAD + CX, count), :] = part
    for y in range(CY):
        for k in range(TILES):
            s[k // 2, W + y, middle, lanes(k)] = own[k, y]
        zs[W + y, middle, :] = own_z[y]

    def outside(low, high, z_low, z_high):
        for k in range(TILES):
            planes = Y_PLANES[k // 2]
            if planes < W:
                s[k // 2, 0, middle, lanes(k)] = jnp.zeros((CX, LANES), F32)
                s[k // 2, NY - 1, middle, lanes(k)] = jnp.zeros((CX, LANES), F32)
            for i in range(planes):
                s[k // 2, W - planes + i, middle, lanes(k)] = low[Y_START[k] + i]
                s[k // 2, W + CY + i, middle, lanes(k)] = high[Y_START[k] + i]
        for i in range(W):
            zs[i, middle, :] = z_low[pl.ds(CX * i, CX), :]
            zs[W + CY + i, middle, :] = z_high[pl.ds(CX * i, CX), :]

    @pl.when(odd == 1)
    def _():
        outside(in_b, in_a, z_b, z_a)

    @pl.when(odd == 0)
    def _():
        outside(in_a, in_b, z_a, z_b)

    narrow = lane_ids((NX, LANES))
    near = (narrow < W) | (narrow >= LANES - W)
    for j in range(NY):
        edges = zs[j]
        for f in range(FIELDS):
            s[f, j, :, 2 * LANES :] = jnp.where(near, pltpu.roll(edges, LANES - (8 * f + W), 1), 0.0)

    wide = lane_ids((NX, span))
    x = lax.broadcasted_iota(jnp.int32, (NX, span), 0)
    inside = jnp.where((x < PAD) & (lax.axis_index("gx") == 0), 0.0, courant_dt)
    inside = jnp.where((wide >= span - W) & (lax.axis_index("gz") == 0), 0.0, inside)
    reach[0] = inside
    reach[1] = inside * (lax.axis_index("gy") > 0).astype(F32)

    def coefs(j, carry):
        phase = s[6, j]

        def chosen(table):
            value = jnp.zeros_like(phase)
            for index in range(4):
                value = jnp.where(phase == index + 1.0, table[index], value)
            return value

        coef[0, j] = chosen(ca_table)
        coef[1, j] = chosen(cb_table)
        coef[2, j] = chosen(sig_table)
        return carry

    lax.fori_loop(0, NY, coefs, 0)

    for step in range(ITERS):
        wave = 60.0 * math.sin(0.6 * (step + 0.5) * courant_dt)

        def magnetic(j):
            ex, ey, ez = s[0, j], s[1, j], s[2, j]
            step_h = reach[0 if j >= W else 1]
            s[3, j] -= step_h * ((s[2, j + 1] - ez) - (pltpu.roll(ey, span - 1, 1) - ey))
            s[4, j] -= step_h * ((pltpu.roll(ex, span - 1, 1) - ex) - (pltpu.roll(ez, NX - 1, 0) - ez))
            s[5, j] -= step_h * ((pltpu.roll(ey, NX - 1, 0) - ey) - (s[0, j + 1] - ex))

        def electric(j):
            hx, hy, hz = s[3, j], s[4, j], s[5, j]
            ca, cb, sig = coef[0, j], coef[1, j], coef[2, j]
            ex = ca * s[0, j] + cb * ((hz - s[5, j - 1]) - (hy - pltpu.roll(hy, 1, 1)))
            ey = ca * s[1, j] + cb * ((hx - pltpu.roll(hx, 1, 1)) - (hz - pltpu.roll(hz, 1, 0)))
            ez = ca * s[2, j] + cb * (((hy - pltpu.roll(hy, 1, 0)) - (hx - s[3, j - 1])) - s[7, j] * wave)
            s[0, j] = ex
            s[1, j] = ey
            s[2, j] = ez
            p = j - W
            if 0 <= p < CY:
                own_z_lanes = slice(0, 2 * LANES)
                ex, ey, ez = ex[:, own_z_lanes], ey[:, own_z_lanes], ez[:, own_z_lanes]
                now = sig[:, own_z_lanes] * (ex * ex + ey * ey + ez * ez)
                power[p] = now if step == 0 else power[p] + now

        magnetic(step)
        for j in range(step + 1, NY - 1 - step):
            magnetic(j)
            electric(j)

    rows = []
    for t in range(TY):
        halves = []
        for k in range(2):
            pair[...] = power[2 * t, :, lanes(k)] + power[2 * t + 1, :, lanes(k)]
            halves.append(pair[pl.ds(PAD, TX, stride=2), :] + pair[pl.ds(PAD + 1, TX, stride=2), :])
        rows.append(jnp.concatenate(halves, axis=1))
    stacked = jnp.concatenate(rows, axis=0)
    source = lax.broadcasted_iota(jnp.int32, (2 * LANES, LANES), 0)
    target = lax.broadcasted_iota(jnp.int32, (2 * LANES, LANES), 1)
    gather = (source // 2 == target).astype(F32)
    summed = jnp.dot(stacked, gather, precision=lax.Precision.HIGHEST, preferred_element_type=F32)
    out[...] = (summed * (1.0 / (8.0 * ITERS))).reshape(TY, TX, LANES)


def beside_z(t):
    wide = lane_ids(t.shape)
    span = t.shape[1]
    ahead = jnp.where(wide == span - 1, 0.0, pltpu.roll(t, span - 1, 1))
    behind = jnp.where(wide == 0, 0.0, pltpu.roll(t, 1, 1))
    return ahead + behind


def beside_x(t, before, after):
    rows = t.shape[0]
    x = lax.broadcasted_iota(jnp.int32, t.shape, 0)
    ahead = jnp.where(x == rows - 1, after, pltpu.roll(t, rows - 1, 0))
    behind = jnp.where(x == 0, before, pltpu.roll(t, 1, 0))
    return ahead + behind


def densified(packing, warmth):
    return packing + 0.3 * (1.0 - packing) * jnp.exp(-3.0 / (1.0 + warmth))


def warm_kernel(warmth, packing, from_below, from_above, z_a, z_b, from_low, from_high, base, packed):
    odd, me = parity(), lax.axis_index("gz")
    tiles = packing.shape[2] // LANES
    t, p, sides, before, after = [], [], [], [], []
    for k in range(tiles):
        near, far = pl.ds(CX * CY + k * TX, TX), pl.ds(CX * W + k * TX, TX)
        low = jnp.where(odd == 1, z_b[far, :], z_a[far, :])
        high = jnp.where(odd == 1, z_a[far, :], z_b[far, :])
        low = jnp.where(me == 0, low, from_below[near, :])
        high = jnp.where(me == lax.axis_size("gz") - 1, high, from_above[near, :])
        sides.append(low + high)
        before.append(from_low[pl.ds(LOW_ROWS + k, 1), :])
        after.append(from_high[pl.ds(HIGH_ROWS + k, 1), :])
        t.append(warmth[pl.ds(k * TX, TX), :])
        p.append(packing[:, 0, pl.ds(k * LANES, LANES)])
    t, p, sides, before, after = (jnp.concatenate(parts, axis=1) for parts in (t, p, sides, before, after))
    lap = beside_x(t, before, after) + sides + beside_z(t) - 6.0 * t
    base[...] = t + 0.1 * ((0.2 + p) * lap)
    packed[...] = densified(p, t)


def first_kernel(base, packed, heat, warmth, density, first, last):
    power = jnp.concatenate([heat[k] for k in range(heat.shape[0])], axis=1)
    t = base[...] + power
    warmth[...] = t
    first[...] = t[:1]
    last[...] = t[TX - 1 :]
    dense = densified(packed[...], t)
    for k in range(heat.shape[0]):
        here = slice(k * LANES, (k + 1) * LANES)
        density[:, 0, here] = dense[:, here]


def second_kernel(warmth, packed, heat, side_a, side_b, before, after, out):
    t = warmth[...]
    lap = beside_x(t, before[...], after[...]) + side_a[...] + side_b[...] + beside_z(t) - 6.0 * t
    grown = t + 0.1 * ((0.2 + packed[...]) * lap)
    for k in range(heat.shape[0]):
        here = slice(k * LANES, (k + 1) * LANES)
        out[:, 0, here] = grown[:, here] + heat[k]


def tile_rows(a):
    lead = a.shape[:-3]
    a = a.reshape(lead + (CX, CY, 2, LANES))
    return jnp.swapaxes(a, -3, -2).reshape(lead + (2 * CX * CY, LANES))


def local(e, h, phase, spots, warmth, packing):
    n_y, n_z, n_x = lax.axis_size("gy"), lax.axis_size("gz"), lax.axis_size("gx")
    across, within = swaps(n_y, 1), swaps(n_y, 0)
    span = warmth.shape[2]
    pencil_rows = TX * span // LANES

    own, to_a, to_b, shared = call(
        pack_kernel,
        (f32(TILES, CY, CX, LANES), f32(Y_TOTAL, CX, LANES), f32(Y_TOTAL, CX, LANES), f32(CX * CY + pencil_rows, LANES)),
        [HBM] * 5,
        scratch=[
            pltpu.SMEM(spots.shape, jnp.int32),
            pltpu.VMEM((3, 2 * CX * CY, LANES), F32),
            pltpu.VMEM((3, 2 * CX * CY, LANES), F32),
            pltpu.VMEM((2 * CX * CY, LANES), jnp.int32),
            pltpu.VMEM(warmth.shape, F32),
            pltpu.SemaphoreType.DMA((9,)),
        ],
        limit=60,
    )(spots, tile_rows(e), tile_rows(h), tile_rows(phase), warmth)
    in_a = lax.ppermute(to_a, "gy", across)
    in_b = lax.ppermute(to_b, "gy", within)
    from_below = lax.ppermute(shared, "gz", [(i, (i + 1) % n_z) for i in range(n_z)])
    from_above = lax.ppermute(shared, "gz", [(i, (i - 1) % n_z) for i in range(n_z)])
    edge = f32(CX * W + pencil_rows, LANES)
    own_z, z_a, z_b = call(edge_kernel, (f32(CY, CX, LANES), edge, edge), [VMEM] * 2)(from_below, from_above)
    z_a = lax.ppermute(z_a, "gy", across)
    z_b = lax.ppermute(z_b, "gy", within)

    def block(rows):
        rows += span // LANES
        return f32(rows + (-rows) % 8, LANES)

    pencil_tiles = shared[CX * CY :]
    to_up, to_down = call(side_kernel, (block(LOW_ROWS), block(HIGH_ROWS)), [VMEM] * 7)(
        own, own_z, in_a, in_b, z_a, z_b, pencil_tiles
    )
    from_low = lax.ppermute(to_up, "gx", shifts(n_x, 1))
    from_high = lax.ppermute(to_down, "gx", shifts(n_x, -1))
    heat = call(
        field_kernel,
        f32(TY, TX, LANES),
        [VMEM] * 8,
        scratch=[
            pltpu.VMEM((FIELDS, NY, NX, 3 * LANES), F32),
            pltpu.VMEM((NY, NX, LANES), F32),
            pltpu.VMEM((3, NY, NX, 3 * LANES), F32),
            pltpu.VMEM((2, NX, 3 * LANES), F32),
            pltpu.VMEM((CY, NX, 2 * LANES), F32),
            pltpu.VMEM((NX, LANES), F32),
        ],
    )(own, own_z, in_a, in_b, z_a, z_b, from_low, from_high)
    heat = lax.all_to_all(heat, "gz", split_axis=0, concat_axis=0, tiled=True)
    pencil, tall, line = f32(TX, span), f32(TX, 1, span), f32(1, span)
    base, packed = call(warm_kernel, (pencil, pencil), [VMEM] * 8)(
        pencil_tiles, packing, from_below, from_above, z_a, z_b, from_low, from_high
    )
    t, density, first, last = call(first_kernel, (pencil, tall, line, line), [VMEM] * 3)(base, packed, heat)
    pencils = n_y * n_z
    side_a = lax.ppermute(t, ("gy", "gz"), swaps(pencils, 1))
    side_b = lax.ppermute(t, ("gy", "gz"), swaps(pencils, 0))
    before = lax.ppermute(last, "gx", shifts(n_x, 1))
    after = lax.ppermute(first, "gx", shifts(n_x, -1))
    result = call(second_kernel, tall, [VMEM] * 7)(t, packed, heat, side_a, side_b, before, after)
    return result, density


def solution(mesh):
    return jax.shard_map(
        local,
        mesh=mesh,
        in_specs=(
            P(None, "gx", "gy", "gz"),
            P(None, "gx", "gy", "gz"),
            P("gx", "gy", "gz"),
            P(("gx", "gy", "gz"), None),
            P("gx", ("gy", "gz"), None),
            P("gx", ("gy", "gz"), None),
        ),
        out_specs=(P("gx", ("gy", "gz"), None), P("gx", ("gy", "gz"), None)),
        check_vma=False,
    )
```

```python
import math

import jax
import jax.numpy as jnp
from jax import lax
from jax.experimental import pallas as pl
from jax.experimental.pallas import tpu as pltpu
from jax.sharding import PartitionSpec as P

ITERS = 4
W = 4
CX, CY, CZ = 16, 8, 256
TX, TY = CX // 2, CY // 2
PAD = W
NX, NY = CX + 2 * PAD, CY + 2 * W
LANES = 128
FIELDS = 8
TILES = 2 * FIELDS

eps_table = (3.0, 9.0, 12.0, 1.0)
sig_table = (0.05, 0.01, 0.4, 0.0)
courant_dt = 0.99 / math.sqrt(3.0)
loss_table = tuple(s * courant_dt / (2.0 * e) for s, e in zip(sig_table, eps_table))
ca_table = tuple((1.0 - l) / (1.0 + l) for l in loss_table)
cb_table = tuple(courant_dt / (e * (1.0 + l)) for l, e in zip(loss_table, eps_table))

F32 = jnp.float32
VMEM = pl.BlockSpec(memory_space=pltpu.VMEM)
HBM = pl.BlockSpec(memory_space=pltpu.HBM)

Y_PLANES = (4, 4, 4, 4, 3, 4, 3, 3)
Y_START = []
for planes in Y_PLANES:
    Y_START += [sum(2 * p for p in Y_PLANES[: len(Y_START) // 2]), 0]
    Y_START[-1] = Y_START[-2] + planes
Y_TOTAL = 2 * sum(Y_PLANES)


def side_rows(low):
    table, place = {}, 0
    for k in range(TILES + 1):
        field = k // 2
        most = W - 1 if field in ((3, 6, 7) if low else (3, 4, 5, 6, 7)) else W
        for j in range(NY):
            corner = W - j if low else j - (W + CY - 1)
            count = min(most, W - corner) if corner > 0 else most
            table[k, j] = (place, count)
            place += count
    return table, place


LOW_TABLE, LOW_ROWS = side_rows(True)
HIGH_TABLE, HIGH_ROWS = side_rows(False)


def f32(*shape):
    return jax.ShapeDtypeStruct(shape, F32)


def call(body, outs, ins, scratch=(), limit=24):
    return pl.pallas_call(
        body,
        out_shape=outs,
        in_specs=ins,
        out_specs=jax.tree.map(lambda _: VMEM, outs),
        scratch_shapes=list(scratch),
        compiler_params=pltpu.CompilerParams(vmem_limit_bytes=limit * 1024 * 1024),
    )


def swaps(size, first):
    pairs = [(i, i + 1) for i in range(first, size - 1, 2)]
    return pairs + [(j, i) for i, j in pairs]


def shifts(size, step):
    return [(i, i + step) for i in range(size) if 0 <= i + step < size]


def lane_ids(shape):
    return lax.broadcasted_iota(jnp.int32, shape, len(shape) - 1)


def parity():
    return lax.rem(lax.axis_index("gy"), 2)


def pack_kernel(spots_hbm, e_hbm, h_hbm, phase_hbm, t_hbm, own, out_a, out_b, shared, spots, e_ref, h_ref, phase_ref, heat, sems):
    odd = parity()
    copies = [
        pltpu.make_async_copy(spots_hbm, spots, sems.at[0]),
        pltpu.make_async_copy(phase_hbm, phase_ref, sems.at[1]),
    ]
    for c in range(3):
        copies.append(pltpu.make_async_copy(e_hbm.at[c], e_ref.at[c], sems.at[2 + c]))
    for c in range(3):
        copies.append(pltpu.make_async_copy(h_hbm.at[c], h_ref.at[c], sems.at[5 + c]))
    copies.append(pltpu.make_async_copy(t_hbm, heat, sems.at[8]))
    for copy in copies:
        copy.start()
    for t in range(2):
        own[14 + t] = jnp.zeros((CY, CX, LANES), F32)

    lane = lane_ids((1, LANES))

    def drop(i, carry):
        spot = spots[0, i]
        x, y = spot >> 11, (spot >> 8) & (CY - 1)
        t, place_z = 14 + ((spot >> 7) & 1), spot & (LANES - 1)
        row = own[t, y, pl.ds(x, 1), :]
        own[t, y, pl.ds(x, 1), :] = row + (lane == place_z).astype(F32)
        return carry

    copies[0].wait()
    lax.fori_loop(0, spots.shape[1], drop, 0)

    def spread(k, source):
        for y in range(CY):
            for t in range(2):
                own[k + t, y] = source[pl.ds(t * CY + y, CX, stride=2 * CY), :].astype(F32)

    copies[1].wait()
    phase_ref[...] += 1
    spread(12, phase_ref)
    for c in range(3):
        copies[2 + c].wait()
        spread(2 * c, e_ref.at[c])
    for c in range(3):
        copies[5 + c].wait()
        spread(2 * (3 + c), h_ref.at[c])
    for k in range(TILES):
        planes = Y_PLANES[k // 2]
        for i in range(planes):
            out_a[Y_START[k] + i] = own[k, odd * (CY - planes) + i]
            out_b[Y_START[k] + i] = own[k, (1 - odd) * (CY - planes) + i]

    wide = lane_ids((CX, LANES))
    slot = wide // 8
    upper = wide % 8 >= W
    for y in range(CY):
        edge = jnp.zeros((CX, LANES), F32)
        for f in range(FIELDS):
            shift = 8 * f + W
            ends = jnp.where(upper, pltpu.roll(own[2 * f, y], shift, 1), pltpu.roll(own[2 * f + 1, y], shift, 1))
            edge = jnp.where(slot == f, ends, edge)
        shared[pl.ds(CX * y, CX), :] = edge
    copies[8].wait()
    for k in range(heat.shape[2] // LANES):
        shared[pl.ds(CX * CY + k * TX, TX), :] = heat[:, 0, pl.ds(k * LANES, LANES)]


def edge_kernel(from_below, from_above, own_z, out_a, out_b):
    odd, me = parity(), lax.axis_index("gz")
    upper = lane_ids((CX, LANES)) % 8 >= W
    has_below = (me > 0).astype(F32)
    has_above = (me < lax.axis_size("gz") - 1).astype(F32)
    for y in range(CY):
        rows = pl.ds(CX * y, CX)
        own_z[y] = jnp.where(upper, from_above[rows, :] * has_above, from_below[rows, :] * has_below)
    thermal = pl.ds(CX * CY, from_below.shape[0] - CX * CY)
    below, above = from_below[thermal, :], from_above[thermal, :]
    for out, up in ((out_a, odd), (out_b, 1 - odd)):
        for i in range(W):
            out[pl.ds(CX * i, CX), :] = own_z[up * (CY - W) + i]
        out[pl.ds(CX * W, thermal.size), :] = jnp.where(up == 1, below, above)


def moved(out, table, up, k, j, rows):
    start, count = table[k, j]
    if count:
        out[pl.ds(start, count), :] = rows[CX - count :] if up else rows[:count]


def middle_kernel(own, own_z, warmth, out_up, out_down):
    for out, table, up in ((out_up, LOW_TABLE, True), (out_down, HIGH_TABLE, False)):
        for k in range(TILES + 1):
            for y in range(CY):
                moved(out, table, up, k, W + y, own_z[y] if k == TILES else own[k, y])
    for k in range(warmth.shape[0] // TX):
        out_up[pl.ds(LOW_ROWS + k, 1), :] = warmth[pl.ds(k * TX + TX - 1, 1), :]
        out_down[pl.ds(HIGH_ROWS + k, 1), :] = warmth[pl.ds(k * TX, 1), :]


def side_kernel(mid_up, mid_down, in_a, in_b, z_a, z_b, out_up, out_down):
    odd = parity()
    out_up[...] = mid_up[...]
    out_down[...] = mid_down[...]

    def outside(low, high, z_low, z_high):
        for out, table, up in ((out_up, LOW_TABLE, True), (out_down, HIGH_TABLE, False)):
            for k in range(TILES):
                planes = Y_PLANES[k // 2]
                for i in range(planes):
                    moved(out, table, up, k, W - planes + i, low[Y_START[k] + i])
                    moved(out, table, up, k, W + CY + i, high[Y_START[k] + i])
            for i in range(W):
                moved(out, table, up, TILES, i, z_low[pl.ds(CX * i, CX), :])
                moved(out, table, up, TILES, W + CY + i, z_high[pl.ds(CX * i, CX), :])

    @pl.when(odd == 1)
    def _():
        outside(in_b, in_a, z_b, z_a)

    @pl.when(odd == 0)
    def _():
        outside(in_a, in_b, z_a, z_b)


def field_kernel(own, own_z, in_a, in_b, z_a, z_b, from_low, from_high, base, out, s, zs, coef, reach, power, pair):
    odd = parity()
    span = 3 * LANES
    middle = pl.ds(PAD, CX)
    outer = (pl.ds(0, PAD), pl.ds(PAD + CX, PAD))

    def lanes(k):
        return pl.ds((k % 2) * LANES, LANES)

    blank = jnp.zeros((PAD, LANES), F32)
    for j in range(NY):
        for rows in outer:
            for k in range(TILES):
                s[k // 2, j, rows, lanes(k)] = blank
            zs[j, rows, :] = blank
        for k in range(TILES + 1):
            start, count = LOW_TABLE[k, j]
            if count:
                part = from_low[pl.ds(start, count), :]
                if k < TILES:
                    s[k // 2, j, pl.ds(PAD - count, count), lanes(k)] = part
                else:
                    zs[j, pl.ds(PAD - count, count), :] = part
            start, count = HIGH_TABLE[k, j]
            if count:
                part = from_high[pl.ds(start, count), :]
                if k < TILES:
                    s[k // 2, j, pl.ds(PAD + CX, count), lanes(k)] = part
                else:
                    zs[j, pl.ds(PAD + CX, count), :] = part
    for y in range(CY):
        for k in range(TILES):
            s[k // 2, W + y, middle, lanes(k)] = own[k, y]
        zs[W + y, middle, :] = own_z[y]

    def outside(low, high, z_low, z_high):
        for k in range(TILES):
            planes = Y_PLANES[k // 2]
            if planes < W:
                s[k // 2, 0, middle, lanes(k)] = jnp.zeros((CX, LANES), F32)
                s[k // 2, NY - 1, middle, lanes(k)] = jnp.zeros((CX, LANES), F32)
            for i in range(planes):
                s[k // 2, W - planes + i, middle, lanes(k)] = low[Y_START[k] + i]
                s[k // 2, W + CY + i, middle, lanes(k)] = high[Y_START[k] + i]
        for i in range(W):
            zs[i, middle, :] = z_low[pl.ds(CX * i, CX), :]
            zs[W + CY + i, middle, :] = z_high[pl.ds(CX * i, CX), :]

    @pl.when(odd == 1)
    def _():
        outside(in_b, in_a, z_b, z_a)

    @pl.when(odd == 0)
    def _():
        outside(in_a, in_b, z_a, z_b)

    narrow = lane_ids((NX, LANES))
    near = (narrow < W) | (narrow >= LANES - W)
    for j in range(NY):
        edges = zs[j]
        for f in range(FIELDS):
            s[f, j, :, 2 * LANES :] = jnp.where(near, pltpu.roll(edges, LANES - (8 * f + W), 1), 0.0)

    wide = lane_ids((NX, span))
    x = lax.broadcasted_iota(jnp.int32, (NX, span), 0)
    inside = jnp.where((x < PAD) & (lax.axis_index("gx") == 0), 0.0, courant_dt)
    inside = jnp.where((wide >= span - W) & (lax.axis_index("gz") == 0), 0.0, inside)
    reach[0] = inside
    reach[1] = inside * (lax.axis_index("gy") > 0).astype(F32)

    def coefs(j, carry):
        phase = s[6, j]

        def chosen(table):
            value = jnp.zeros_like(phase)
            for index in range(4):
                value = jnp.where(phase == index + 1.0, table[index], value)
            return value

        coef[0, j] = chosen(ca_table)
        coef[1, j] = chosen(cb_table)
        coef[2, j] = chosen(sig_table)
        return carry

    lax.fori_loop(0, NY, coefs, 0)

    for step in range(ITERS):
        wave = 60.0 * math.sin(0.6 * (step + 0.5) * courant_dt)

        def magnetic(j):
            ex, ey, ez = s[0, j], s[1, j], s[2, j]
            step_h = reach[0 if j >= W else 1]
            s[3, j] -= step_h * ((s[2, j + 1] - ez) - (pltpu.roll(ey, span - 1, 1) - ey))
            s[4, j] -= step_h * ((pltpu.roll(ex, span - 1, 1) - ex) - (pltpu.roll(ez, NX - 1, 0) - ez))
            s[5, j] -= step_h * ((pltpu.roll(ey, NX - 1, 0) - ey) - (s[0, j + 1] - ex))

        def electric(j):
            hx, hy, hz = s[3, j], s[4, j], s[5, j]
            ca, cb, sig = coef[0, j], coef[1, j], coef[2, j]
            ex = ca * s[0, j] + cb * ((hz - s[5, j - 1]) - (hy - pltpu.roll(hy, 1, 1)))
            ey = ca * s[1, j] + cb * ((hx - pltpu.roll(hx, 1, 1)) - (hz - pltpu.roll(hz, 1, 0)))
            ez = ca * s[2, j] + cb * (((hy - pltpu.roll(hy, 1, 0)) - (hx - s[3, j - 1])) - s[7, j] * wave)
            s[0, j] = ex
            s[1, j] = ey
            s[2, j] = ez
            p = j - W
            if 0 <= p < CY:
                own_z_lanes = slice(0, 2 * LANES)
                ex, ey, ez = ex[:, own_z_lanes], ey[:, own_z_lanes], ez[:, own_z_lanes]
                now = sig[:, own_z_lanes] * (ex * ex + ey * ey + ez * ez)
                power[p] = now if step == 0 else power[p] + now

        magnetic(step)
        for j in range(step + 1, NY - 1 - step):
            magnetic(j)
            electric(j)

    rows = []
    for t in range(TY):
        halves = []
        for k in range(2):
            pair[...] = power[2 * t, :, lanes(k)] + power[2 * t + 1, :, lanes(k)]
            halves.append(pair[pl.ds(PAD, TX, stride=2), :] + pair[pl.ds(PAD + 1, TX, stride=2), :])
        rows.append(jnp.concatenate(halves, axis=1))
    stacked = jnp.concatenate(rows, axis=0)
    source = lax.broadcasted_iota(jnp.int32, (2 * LANES, LANES), 0)
    target = lax.broadcasted_iota(jnp.int32, (2 * LANES, LANES), 1)
    gather = (source // 2 == target).astype(F32)
    summed = jnp.dot(stacked, gather, precision=lax.Precision.HIGHEST, preferred_element_type=F32)
    summed = summed * (1.0 / (8.0 * ITERS))
    for d in range(TY):
        for i, t in enumerate((d - 1, d, d + 1)):
            out[d, i] = summed[TX * t : TX * (t + 1)] if 0 <= t < TY else jnp.zeros((TX, LANES), F32)
        for k in range(base.shape[1] // LANES):
            out[d, 3 + k] = base[:, pl.ds(k * LANES, LANES)]


def beside_z(t):
    wide = lane_ids(t.shape)
    span = t.shape[1]
    ahead = jnp.where(wide == span - 1, 0.0, pltpu.roll(t, span - 1, 1))
    behind = jnp.where(wide == 0, 0.0, pltpu.roll(t, 1, 1))
    return ahead + behind


def beside_x(t, before, after):
    rows = t.shape[0]
    x = lax.broadcasted_iota(jnp.int32, t.shape, 0)
    ahead = jnp.where(x == rows - 1, after, pltpu.roll(t, rows - 1, 0))
    behind = jnp.where(x == 0, before, pltpu.roll(t, 1, 0))
    return ahead + behind


def densified(packing, warmth):
    return packing + 0.3 * (1.0 - packing) * jnp.exp(-3.0 / (1.0 + warmth))


def warm_kernel(warmth, packing, from_below, from_above, z_a, z_b, from_low, from_high, base, packed):
    odd, me = parity(), lax.axis_index("gz")
    tiles = packing.shape[2] // LANES
    t, p, sides, before, after = [], [], [], [], []
    for k in range(tiles):
        near, far = pl.ds(CX * CY + k * TX, TX), pl.ds(CX * W + k * TX, TX)
        low = jnp.where(odd == 1, z_b[far, :], z_a[far, :])
        high = jnp.where(odd == 1, z_a[far, :], z_b[far, :])
        low = jnp.where(me == 0, low, from_below[near, :])
        high = jnp.where(me == lax.axis_size("gz") - 1, high, from_above[near, :])
        sides.append(low + high)
        before.append(from_low[pl.ds(LOW_ROWS + k, 1), :])
        after.append(from_high[pl.ds(HIGH_ROWS + k, 1), :])
        t.append(warmth[pl.ds(k * TX, TX), :])
        p.append(packing[:, 0, pl.ds(k * LANES, LANES)])
    t, p, sides, before, after = (jnp.concatenate(parts, axis=1) for parts in (t, p, sides, before, after))
    lap = beside_x(t, before, after) + sides + beside_z(t) - 6.0 * t
    base[...] = t + 0.1 * ((0.2 + p) * lap)
    packed[...] = densified(p, t)


def first_kernel(base, heat, warmth, beside, first, last):
    me = lax.axis_index("gz")
    tiles = heat.shape[0]
    has_low = (me > 0).astype(F32)
    has_high = (me < tiles - 1).astype(F32)
    low, high = jnp.maximum(me - 1, 0), jnp.minimum(me + 1, tiles - 1)
    for k in range(tiles):
        lanes = pl.ds(k * LANES, LANES)
        t = base[:, lanes] + heat[k, 1]
        warmth[:, lanes] = t
        first[:, lanes] = t[:1]
        last[:, lanes] = t[TX - 1 :]
        below = (heat[low, 3 + k] + heat[k, 0]) * has_low
        above = (heat[high, 3 + k] + heat[k, 2]) * has_high
        beside[:, lanes] = below + above


def dense_kernel(packed, warmth, density):
    dense = densified(packed[...], warmth[...])
    for k in range(dense.shape[1] // LANES):
        here = slice(k * LANES, (k + 1) * LANES)
        density[:, 0, here] = dense[:, here]


def second_kernel(warmth, packed, heat, beside, across, before, after, out):
    t = warmth[...]
    lap = beside_x(t, before[...], after[...]) + beside[...] + across[...] + beside_z(t) - 6.0 * t
    grown = t + 0.1 * ((0.2 + packed[...]) * lap)
    for k in range(heat.shape[0]):
        here = slice(k * LANES, (k + 1) * LANES)
        out[:, 0, here] = grown[:, here] + heat[k, 1]


def tile_rows(a):
    lead = a.shape[:-3]
    a = a.reshape(lead + (CX, CY, 2, LANES))
    return jnp.swapaxes(a, -3, -2).reshape(lead + (2 * CX * CY, LANES))


def local(e, h, phase, spots, warmth, packing):
    n_y, n_z, n_x = lax.axis_size("gy"), lax.axis_size("gz"), lax.axis_size("gx")
    across, within = swaps(n_y, 1), swaps(n_y, 0)
    span = warmth.shape[2]
    pencil_rows = TX * span // LANES

    own, to_a, to_b, shared = call(
        pack_kernel,
        (f32(TILES, CY, CX, LANES), f32(Y_TOTAL, CX, LANES), f32(Y_TOTAL, CX, LANES), f32(CX * CY + pencil_rows, LANES)),
        [HBM] * 5,
        scratch=[
            pltpu.SMEM(spots.shape, jnp.int32),
            pltpu.VMEM((3, 2 * CX * CY, LANES), F32),
            pltpu.VMEM((3, 2 * CX * CY, LANES), F32),
            pltpu.VMEM((2 * CX * CY, LANES), jnp.int32),
            pltpu.VMEM(warmth.shape, F32),
            pltpu.SemaphoreType.DMA((9,)),
        ],
        limit=60,
    )(spots, tile_rows(e), tile_rows(h), tile_rows(phase), warmth)
    in_a = lax.ppermute(to_a, "gy", across)
    in_b = lax.ppermute(to_b, "gy", within)
    from_below = lax.ppermute(shared, "gz", [(i, (i + 1) % n_z) for i in range(n_z)])
    from_above = lax.ppermute(shared, "gz", [(i, (i - 1) % n_z) for i in range(n_z)])
    edge = f32(CX * W + pencil_rows, LANES)
    own_z, z_a, z_b = call(edge_kernel, (f32(CY, CX, LANES), edge, edge), [VMEM] * 2)(from_below, from_above)
    z_a = lax.ppermute(z_a, "gy", across)
    z_b = lax.ppermute(z_b, "gy", within)

    def block(rows):
        rows += span // LANES
        return f32(rows + (-rows) % 8, LANES)

    pencil_tiles = shared[CX * CY :]
    blocks = (block(LOW_ROWS), block(HIGH_ROWS))
    middle = call(middle_kernel, blocks, [VMEM] * 3)(own, own_z, pencil_tiles)
    to_up, to_down = call(side_kernel, blocks, [VMEM] * 6)(*middle, in_a, in_b, z_a, z_b)
    from_low = lax.ppermute(to_up, "gx", shifts(n_x, 1))
    from_high = lax.ppermute(to_down, "gx", shifts(n_x, -1))
    pencil, tall, line = f32(TX, span), f32(TX, 1, span), f32(1, span)
    base, packed = call(warm_kernel, (pencil, pencil), [VMEM] * 8)(
        pencil_tiles, packing, from_below, from_above, z_a, z_b, from_low, from_high
    )
    heat = call(
        field_kernel,
        f32(TY, 3 + span // LANES, TX, LANES),
        [VMEM] * 9,
        scratch=[
            pltpu.VMEM((FIELDS, NY, NX, 3 * LANES), F32),
            pltpu.VMEM((NY, NX, LANES), F32),
            pltpu.VMEM((3, NY, NX, 3 * LANES), F32),
            pltpu.VMEM((2, NX, 3 * LANES), F32),
            pltpu.VMEM((CY, NX, 2 * LANES), F32),
            pltpu.VMEM((NX, LANES), F32),
        ],
    )(own, own_z, in_a, in_b, z_a, z_b, from_low, from_high, base)
    heat = lax.all_to_all(heat, "gz", split_axis=0, concat_axis=0, tiled=True)
    t, beside, first, last = call(first_kernel, (pencil, pencil, line, line), [VMEM] * 2)(base, heat)
    ends = [(i, i + 1) for i in range(n_z - 1, n_y * n_z - 1, n_z)]
    outer = lax.ppermute(t, ("gy", "gz"), ends + [(j, i) for i, j in ends])
    before = lax.ppermute(last, "gx", shifts(n_x, 1))
    after = lax.ppermute(first, "gx", shifts(n_x, -1))
    density = call(dense_kernel, tall, [VMEM] * 2)(packed, t)
    result = call(second_kernel, tall, [VMEM] * 7)(t, packed, heat, beside, outer, before, after)
    return result, density


def solution(mesh):
    return jax.shard_map(
        local,
        mesh=mesh,
        in_specs=(
            P(None, "gx", "gy", "gz"),
            P(None, "gx", "gy", "gz"),
            P("gx", "gy", "gz"),
            P(("gx", "gy", "gz"), None),
            P("gx", ("gy", "gz"), None),
            P("gx", ("gy", "gz"), None),
        ),
        out_specs=(P("gx", ("gy", "gz"), None), P("gx", ("gy", "gz"), None)),
        check_vma=False,
    )
```

```python
import math

import jax
import jax.numpy as jnp
from jax import lax
from jax.experimental import pallas as pl
from jax.experimental.pallas import tpu as pltpu
from jax.sharding import PartitionSpec as P

ITERS = 4
W = 4
CX, CY, CZ = 16, 8, 256
TX, TY = CX // 2, CY // 2
NY = CY + 2 * W
LANES = 128
FIELDS = 8
TILES = 2 * FIELDS

eps_table = (3.0, 9.0, 12.0, 1.0)
sig_table = (0.05, 0.01, 0.4, 0.0)
courant_dt = 0.99 / math.sqrt(3.0)
loss_table = tuple(s * courant_dt / (2.0 * e) for s, e in zip(sig_table, eps_table))
ca_table = tuple((1.0 - l) / (1.0 + l) for l in loss_table)
cb_table = tuple(courant_dt / (e * (1.0 + l)) for l, e in zip(loss_table, eps_table))

F32 = jnp.float32
VMEM = pl.BlockSpec(memory_space=pltpu.VMEM)
HBM = pl.BlockSpec(memory_space=pltpu.HBM)

Y_PLANES = (4, 4, 4, 4, 3, 4, 3, 3)
Y_START = []
for planes in Y_PLANES:
    Y_START += [sum(2 * p for p in Y_PLANES[: len(Y_START) // 2]), 0]
    Y_START[-1] = Y_START[-2] + planes
Y_TOTAL = 2 * sum(Y_PLANES)


def side_rows(low):
    table, place = {}, 0
    for k in range(TILES + 1):
        field = k // 2
        most = W - 1 if field in ((3, 6, 7) if low else (3, 4, 5, 6, 7)) else W
        for j in range(NY):
            corner = W - j if low else j - (W + CY - 1)
            count = min(most, W - corner) if corner > 0 else most
            table[k, j] = (place, count)
            place += count
    return table, place


LOW_TABLE, LOW_ROWS = side_rows(True)
HIGH_TABLE, HIGH_ROWS = side_rows(False)


def f32(*shape):
    return jax.ShapeDtypeStruct(shape, F32)


def call(body, outs, ins, scratch=(), limit=24):
    return pl.pallas_call(
        body,
        out_shape=outs,
        in_specs=ins,
        out_specs=jax.tree.map(lambda _: VMEM, outs),
        scratch_shapes=list(scratch),
        compiler_params=pltpu.CompilerParams(vmem_limit_bytes=limit * 1024 * 1024),
    )


def swaps(size, first):
    pairs = [(i, i + 1) for i in range(first, size - 1, 2)]
    return pairs + [(j, i) for i, j in pairs]


def shifts(size, step):
    return [(i, i + step) for i in range(size) if 0 <= i + step < size]


def lane_ids(shape):
    return lax.broadcasted_iota(jnp.int32, shape, len(shape) - 1)


def parity():
    return lax.rem(lax.axis_index("gy"), 2)


def pack_kernel(spots_hbm, e_hbm, h_hbm, phase_hbm, t_hbm, own, out_a, out_b, shared, spots, e_ref, h_ref, phase_ref, heat, sems):
    odd = parity()
    copies = [
        pltpu.make_async_copy(spots_hbm, spots, sems.at[0]),
        pltpu.make_async_copy(phase_hbm, phase_ref, sems.at[1]),
    ]
    for c in range(3):
        copies.append(pltpu.make_async_copy(e_hbm.at[c], e_ref.at[c], sems.at[2 + c]))
    for c in range(3):
        copies.append(pltpu.make_async_copy(h_hbm.at[c], h_ref.at[c], sems.at[5 + c]))
    copies.append(pltpu.make_async_copy(t_hbm, heat, sems.at[8]))
    for copy in copies:
        copy.start()
    for t in range(2):
        own[14 + t] = jnp.zeros((CY, CX, LANES), F32)

    lane = lane_ids((1, LANES))

    def drop(i, carry):
        spot = spots[0, i]
        x, y = spot >> 11, (spot >> 8) & (CY - 1)
        t, place_z = 14 + ((spot >> 7) & 1), spot & (LANES - 1)
        row = own[t, y, pl.ds(x, 1), :]
        own[t, y, pl.ds(x, 1), :] = row + (lane == place_z).astype(F32)
        return carry

    copies[0].wait()
    lax.fori_loop(0, spots.shape[1], drop, 0)

    def spread(k, source):
        for y in range(CY):
            for t in range(2):
                own[k + t, y] = source[pl.ds(t * CY + y, CX, stride=2 * CY), :].astype(F32)

    copies[1].wait()
    phase_ref[...] += 1
    spread(12, phase_ref)
    for c in range(3):
        copies[2 + c].wait()
        spread(2 * c, e_ref.at[c])
    for c in range(3):
        copies[5 + c].wait()
        spread(2 * (3 + c), h_ref.at[c])
    for k in range(TILES):
        planes = Y_PLANES[k // 2]
        for i in range(planes):
            out_a[Y_START[k] + i] = own[k, odd * (CY - planes) + i]
            out_b[Y_START[k] + i] = own[k, (1 - odd) * (CY - planes) + i]

    wide = lane_ids((CX, LANES))
    slot = wide // 8
    upper = wide % 8 >= W
    for y in range(CY):
        edge = jnp.zeros((CX, LANES), F32)
        for f in range(FIELDS):
            shift = 8 * f + W
            ends = jnp.where(upper, pltpu.roll(own[2 * f, y], shift, 1), pltpu.roll(own[2 * f + 1, y], shift, 1))
            edge = jnp.where(slot == f, ends, edge)
        shared[pl.ds(CX * y, CX), :] = edge
    copies[8].wait()
    for k in range(heat.shape[2] // LANES):
        shared[pl.ds(CX * CY + k * TX, TX), :] = heat[:, 0, pl.ds(k * LANES, LANES)]


def edge_kernel(from_below, from_above, own_z, out_a, out_b):
    odd, me = parity(), lax.axis_index("gz")
    upper = lane_ids((CX, LANES)) % 8 >= W
    has_below = (me > 0).astype(F32)
    has_above = (me < lax.axis_size("gz") - 1).astype(F32)
    for y in range(CY):
        rows = pl.ds(CX * y, CX)
        own_z[y] = jnp.where(upper, from_above[rows, :] * has_above, from_below[rows, :] * has_below)
    thermal = pl.ds(CX * CY, from_below.shape[0] - CX * CY)
    below, above = from_below[thermal, :], from_above[thermal, :]
    for out, up in ((out_a, odd), (out_b, 1 - odd)):
        for i in range(W):
            out[pl.ds(CX * i, CX), :] = own_z[up * (CY - W) + i]
        out[pl.ds(CX * W, thermal.size), :] = jnp.where(up == 1, below, above)


def moved(out, table, up, k, j, rows):
    start, count = table[k, j]
    if count:
        out[pl.ds(start, count), :] = rows[CX - count :] if up else rows[:count]


def middle_kernel(own, own_z, warmth, out_up, out_down):
    for out, table, up in ((out_up, LOW_TABLE, True), (out_down, HIGH_TABLE, False)):
        for k in range(TILES + 1):
            for y in range(CY):
                moved(out, table, up, k, W + y, own_z[y] if k == TILES else own[k, y])
    for k in range(warmth.shape[0] // TX):
        out_up[pl.ds(LOW_ROWS + k, 1), :] = warmth[pl.ds(k * TX + TX - 1, 1), :]
        out_down[pl.ds(HIGH_ROWS + k, 1), :] = warmth[pl.ds(k * TX, 1), :]


def side_kernel(mid_up, mid_down, in_a, in_b, z_a, z_b, out_up, out_down):
    odd = parity()
    out_up[...] = mid_up[...]
    out_down[...] = mid_down[...]

    def outside(low, high, z_low, z_high):
        for out, table, up in ((out_up, LOW_TABLE, True), (out_down, HIGH_TABLE, False)):
            for k in range(TILES):
                planes = Y_PLANES[k // 2]
                for i in range(planes):
                    moved(out, table, up, k, W - planes + i, low[Y_START[k] + i])
                    moved(out, table, up, k, W + CY + i, high[Y_START[k] + i])
            for i in range(W):
                moved(out, table, up, TILES, i, z_low[pl.ds(CX * i, CX), :])
                moved(out, table, up, TILES, W + CY + i, z_high[pl.ds(CX * i, CX), :])

    @pl.when(odd == 1)
    def _():
        outside(in_b, in_a, z_b, z_a)

    @pl.when(odd == 0)
    def _():
        outside(in_a, in_b, z_a, z_b)


HALF = CX // 2


def planes_of(own, own_z, in_a, in_b, z_a, z_b, put):
    for y in range(CY):
        for k in range(TILES):
            put(k, W + y, own[k, y])
        put(TILES, W + y, own_z[y])

    def outside(low, high, z_low, z_high):
        for k in range(TILES):
            planes = Y_PLANES[k // 2]
            if planes < W:
                put(k, 0, jnp.zeros((CX, LANES), F32))
                put(k, NY - 1, jnp.zeros((CX, LANES), F32))
            for i in range(planes):
                put(k, W - planes + i, low[Y_START[k] + i])
                put(k, W + CY + i, high[Y_START[k] + i])
        for i in range(W):
            put(TILES, i, z_low[pl.ds(CX * i, CX), :])
            put(TILES, W + CY + i, z_high[pl.ds(CX * i, CX), :])

    @pl.when(parity() == 1)
    def _():
        outside(in_b, in_a, z_b, z_a)

    @pl.when(parity() == 0)
    def _():
        outside(in_a, in_b, z_a, z_b)


def half_lanes(k):
    return pl.ds((k % 2) * LANES, LANES)


def leapfrog(s, zs, coef, reach, power, keep, middle):
    span = 3 * LANES
    narrow = lane_ids((CX, LANES))
    near = (narrow < W) | (narrow >= LANES - W)
    for j in range(NY):
        edges = zs[j]
        for f in range(FIELDS):
            s[f, j, :, 2 * LANES :] = jnp.where(near, pltpu.roll(edges, LANES - (8 * f + W), 1), 0.0)

    wide = lane_ids((CX, span))
    x = lax.broadcasted_iota(jnp.int32, (CX, span), 0)
    inside = jnp.full((CX, span), courant_dt, F32)
    if not middle:
        inside = jnp.where((x < W) & (lax.axis_index("gx") == 0), 0.0, inside)
    inside = jnp.where((wide >= span - W) & (lax.axis_index("gz") == 0), 0.0, inside)
    reach[0] = inside
    reach[1] = inside * (lax.axis_index("gy") > 0).astype(F32)

    def coefs(j, carry):
        phase = s[6, j]

        def chosen(table):
            value = jnp.zeros_like(phase)
            for index in range(4):
                value = jnp.where(phase == index + 1.0, table[index], value)
            return value

        coef[0, j] = chosen(ca_table)
        coef[1, j] = chosen(cb_table)
        coef[2, j] = chosen(sig_table)
        return carry

    lax.fori_loop(0, NY, coefs, 0)

    for step in range(ITERS):
        wave = 60.0 * math.sin(0.6 * (step + 0.5) * courant_dt)

        def ahead_x(value, q, j):
            turned = pltpu.roll(value, CX - 1, 0)
            if middle:
                keep[step, q, pl.ds(j, 1), :] = value[W : W + 1]
                return turned
            return jnp.where(x == HALF - 1, keep[step, q, pl.ds(j, 1), :], turned)

        def behind_x(value, q, j):
            turned = pltpu.roll(value, 1, 0)
            if middle:
                keep[step, q, pl.ds(j, 1), :] = value[CX - W - 1 : CX - W]
                return turned
            return jnp.where(x == HALF, keep[step, q, pl.ds(j, 1), :], turned)

        def magnetic(j):
            ex, ey, ez = s[0, j], s[1, j], s[2, j]
            step_h = reach[0 if j >= W else 1]
            s[3, j] -= step_h * ((s[2, j + 1] - ez) - (pltpu.roll(ey, span - 1, 1) - ey))
            s[4, j] -= step_h * ((pltpu.roll(ex, span - 1, 1) - ex) - (ahead_x(ez, 1, j) - ez))
            s[5, j] -= step_h * ((ahead_x(ey, 0, j) - ey) - (s[0, j + 1] - ex))

        def electric(j):
            hx, hy, hz = s[3, j], s[4, j], s[5, j]
            ca, cb, sig = coef[0, j], coef[1, j], coef[2, j]
            ex = ca * s[0, j] + cb * ((hz - s[5, j - 1]) - (hy - pltpu.roll(hy, 1, 1)))
            ey = ca * s[1, j] + cb * ((hx - pltpu.roll(hx, 1, 1)) - (hz - behind_x(hz, 3, j)))
            ez = ca * s[2, j] + cb * (((hy - behind_x(hy, 2, j)) - (hx - s[3, j - 1])) - s[7, j] * wave)
            s[0, j] = ex
            s[1, j] = ey
            s[2, j] = ez
            p = j - W
            if 0 <= p < CY:
                own = slice(0, 2 * LANES)
                ex, ey, ez = ex[:, own], ey[:, own], ez[:, own]
                now = sig[:, own] * (ex * ex + ey * ey + ez * ez)
                power[p] = now if step == 0 else power[p] + now

        magnetic(step)
        for j in range(step + 1, NY - 1 - step):
            magnetic(j)
            electric(j)


def middle_field_kernel(own, own_z, in_a, in_b, z_a, z_b, power, keep, s, zs, coef, reach):
    def put(k, j, rows):
        if k == TILES:
            zs[j] = rows
        else:
            s[k // 2, j, :, half_lanes(k)] = rows

    planes_of(own, own_z, in_a, in_b, z_a, z_b, put)
    leapfrog(s, zs, coef, reach, power, keep, True)


def field_kernel(own, own_z, in_a, in_b, z_a, z_b, from_low, from_high, base, inner, keep, out, s, zs, coef, reach, power, pair):
    def store(k, j, start, rows):
        here = pl.ds(start, rows.shape[0])
        if k == TILES:
            zs[j, here, :] = rows
        else:
            s[k // 2, j, here, half_lanes(k)] = rows

    for j in range(NY):
        for k in range(TILES + 1):
            for message, table, edge in ((from_low, LOW_TABLE, 0), (from_high, HIGH_TABLE, CX - W)):
                start, count = table[k, j]
                if count < W:
                    store(k, j, edge, jnp.zeros((W, LANES), F32))
                if count:
                    store(k, j, W - count if edge == 0 else edge, message[pl.ds(start, count), :])

    def put(k, j, rows):
        store(k, j, W, rows[:W])
        store(k, j, HALF, rows[CX - W :])

    planes_of(own, own_z, in_a, in_b, z_a, z_b, put)
    leapfrog(s, zs, coef, reach, power, keep, False)

    rows = []
    for t in range(TY):
        halves = []
        for k in range(2):
            lanes = half_lanes(k)
            ends = power[2 * t, :, lanes] + power[2 * t + 1, :, lanes]
            centre = inner[2 * t, :, lanes] + inner[2 * t + 1, :, lanes]
            pair[pl.ds(0, W), :] = ends[W : 2 * W]
            pair[pl.ds(W, HALF), :] = centre[W : W + HALF]
            pair[pl.ds(W + HALF, W), :] = ends[HALF : HALF + W]
            halves.append(pair[pl.ds(0, TX, stride=2), :] + pair[pl.ds(1, TX, stride=2), :])
        rows.append(jnp.concatenate(halves, axis=1))
    stacked = jnp.concatenate(rows, axis=0)
    source = lax.broadcasted_iota(jnp.int32, (2 * LANES, LANES), 0)
    target = lax.broadcasted_iota(jnp.int32, (2 * LANES, LANES), 1)
    gather = (source // 2 == target).astype(F32)
    summed = jnp.dot(stacked, gather, precision=lax.Precision.HIGHEST, preferred_element_type=F32)
    summed = summed * (1.0 / (8.0 * ITERS))
    for d in range(TY):
        for i, t in enumerate((d - 1, d, d + 1)):
            out[d, i] = summed[TX * t : TX * (t + 1)] if 0 <= t < TY else jnp.zeros((TX, LANES), F32)
        for k in range(base.shape[1] // LANES):
            out[d, 3 + k] = base[:, pl.ds(k * LANES, LANES)]


def beside_z(t):
    wide = lane_ids(t.shape)
    span = t.shape[1]
    ahead = jnp.where(wide == span - 1, 0.0, pltpu.roll(t, span - 1, 1))
    behind = jnp.where(wide == 0, 0.0, pltpu.roll(t, 1, 1))
    return ahead + behind


def beside_x(t, before, after):
    rows = t.shape[0]
    x = lax.broadcasted_iota(jnp.int32, t.shape, 0)
    ahead = jnp.where(x == rows - 1, after, pltpu.roll(t, rows - 1, 0))
    behind = jnp.where(x == 0, before, pltpu.roll(t, 1, 0))
    return ahead + behind


def densified(packing, warmth):
    return packing + 0.3 * (1.0 - packing) * jnp.exp(-3.0 / (1.0 + warmth))


def warm_kernel(warmth, packing, from_below, from_above, z_a, z_b, from_low, from_high, base, packed):
    odd, me = parity(), lax.axis_index("gz")
    tiles = packing.shape[2] // LANES
    t, p, sides, before, after = [], [], [], [], []
    for k in range(tiles):
        near, far = pl.ds(CX * CY + k * TX, TX), pl.ds(CX * W + k * TX, TX)
        low = jnp.where(odd == 1, z_b[far, :], z_a[far, :])
        high = jnp.where(odd == 1, z_a[far, :], z_b[far, :])
        low = jnp.where(me == 0, low, from_below[near, :])
        high = jnp.where(me == lax.axis_size("gz") - 1, high, from_above[near, :])
        sides.append(low + high)
        before.append(from_low[pl.ds(LOW_ROWS + k, 1), :])
        after.append(from_high[pl.ds(HIGH_ROWS + k, 1), :])
        t.append(warmth[pl.ds(k * TX, TX), :])
        p.append(packing[:, 0, pl.ds(k * LANES, LANES)])
    t, p, sides, before, after = (jnp.concatenate(parts, axis=1) for parts in (t, p, sides, before, after))
    lap = beside_x(t, before, after) + sides + beside_z(t) - 6.0 * t
    base[...] = t + 0.1 * ((0.2 + p) * lap)
    packed[...] = densified(p, t)


def first_kernel(base, heat, warmth, beside, first, last):
    me = lax.axis_index("gz")
    tiles = heat.shape[0]
    has_low = (me > 0).astype(F32)
    has_high = (me < tiles - 1).astype(F32)
    low, high = jnp.maximum(me - 1, 0), jnp.minimum(me + 1, tiles - 1)
    for k in range(tiles):
        lanes = pl.ds(k * LANES, LANES)
        t = base[:, lanes] + heat[k, 1]
        warmth[:, lanes] = t
        first[:, lanes] = t[:1]
        last[:, lanes] = t[TX - 1 :]
        below = (heat[low, 3 + k] + heat[k, 0]) * has_low
        above = (heat[high, 3 + k] + heat[k, 2]) * has_high
        beside[:, lanes] = below + above


def dense_kernel(packed, warmth, density):
    dense = densified(packed[...], warmth[...])
    for k in range(dense.shape[1] // LANES):
        here = slice(k * LANES, (k + 1) * LANES)
        density[:, 0, here] = dense[:, here]


def second_kernel(warmth, packed, heat, beside, across, before, after, out):
    t = warmth[...]
    lap = beside_x(t, before[...], after[...]) + beside[...] + across[...] + beside_z(t) - 6.0 * t
    grown = t + 0.1 * ((0.2 + packed[...]) * lap)
    for k in range(heat.shape[0]):
        here = slice(k * LANES, (k + 1) * LANES)
        out[:, 0, here] = grown[:, here] + heat[k, 1]


def tile_rows(a):
    lead = a.shape[:-3]
    a = a.reshape(lead + (CX, CY, 2, LANES))
    return jnp.swapaxes(a, -3, -2).reshape(lead + (2 * CX * CY, LANES))


def local(e, h, phase, spots, warmth, packing):
    n_y, n_z, n_x = lax.axis_size("gy"), lax.axis_size("gz"), lax.axis_size("gx")
    across, within = swaps(n_y, 1), swaps(n_y, 0)
    span = warmth.shape[2]
    pencil_rows = TX * span // LANES

    own, to_a, to_b, shared = call(
        pack_kernel,
        (f32(TILES, CY, CX, LANES), f32(Y_TOTAL, CX, LANES), f32(Y_TOTAL, CX, LANES), f32(CX * CY + pencil_rows, LANES)),
        [HBM] * 5,
        scratch=[
            pltpu.SMEM(spots.shape, jnp.int32),
            pltpu.VMEM((3, 2 * CX * CY, LANES), F32),
            pltpu.VMEM((3, 2 * CX * CY, LANES), F32),
            pltpu.VMEM((2 * CX * CY, LANES), jnp.int32),
            pltpu.VMEM(warmth.shape, F32),
            pltpu.SemaphoreType.DMA((9,)),
        ],
        limit=60,
    )(spots, tile_rows(e), tile_rows(h), tile_rows(phase), warmth)
    in_a = lax.ppermute(to_a, "gy", across)
    in_b = lax.ppermute(to_b, "gy", within)
    from_below = lax.ppermute(shared, "gz", [(i, (i + 1) % n_z) for i in range(n_z)])
    from_above = lax.ppermute(shared, "gz", [(i, (i - 1) % n_z) for i in range(n_z)])
    edge = f32(CX * W + pencil_rows, LANES)
    own_z, z_a, z_b = call(edge_kernel, (f32(CY, CX, LANES), edge, edge), [VMEM] * 2)(from_below, from_above)
    z_a = lax.ppermute(z_a, "gy", across)
    z_b = lax.ppermute(z_b, "gy", within)

    def block(rows):
        rows += span // LANES
        return f32(rows + (-rows) % 8, LANES)

    pencil_tiles = shared[CX * CY :]
    blocks = (block(LOW_ROWS), block(HIGH_ROWS))
    middle = call(middle_kernel, blocks, [VMEM] * 3)(own, own_z, pencil_tiles)
    to_up, to_down = call(side_kernel, blocks, [VMEM] * 6)(*middle, in_a, in_b, z_a, z_b)
    from_low = lax.ppermute(to_up, "gx", shifts(n_x, 1))
    from_high = lax.ppermute(to_down, "gx", shifts(n_x, -1))
    pencil, tall, line = f32(TX, span), f32(TX, 1, span), f32(1, span)
    base, packed = call(warm_kernel, (pencil, pencil), [VMEM] * 8)(
        pencil_tiles, packing, from_below, from_above, z_a, z_b, from_low, from_high
    )
    work = [
        pltpu.VMEM((FIELDS, NY, CX, 3 * LANES), F32),
        pltpu.VMEM((NY, CX, LANES), F32),
        pltpu.VMEM((3, NY, CX, 3 * LANES), F32),
        pltpu.VMEM((2, CX, 3 * LANES), F32),
    ]
    power = (CY, CX, 2 * LANES)
    local_parts = (own, own_z, in_a, in_b, z_a, z_b)
    inner = call(middle_field_kernel, (f32(*power), f32(ITERS, 4, NY, 3 * LANES)), [VMEM] * 6, scratch=work)(*local_parts)
    heat = call(
        field_kernel,
        f32(TY, 3 + span // LANES, TX, LANES),
        [VMEM] * 11,
        scratch=work + [pltpu.VMEM(power, F32), pltpu.VMEM((CX, LANES), F32)],
    )(*local_parts, from_low, from_high, base, *inner)
    heat = lax.all_to_all(heat, "gz", split_axis=0, concat_axis=0, tiled=True)
    t, beside, first, last = call(first_kernel, (pencil, pencil, line, line), [VMEM] * 2)(base, heat)
    ends = [(i, i + 1) for i in range(n_z - 1, n_y * n_z - 1, n_z)]
    outer = lax.ppermute(t, ("gy", "gz"), ends + [(j, i) for i, j in ends])
    before = lax.ppermute(last, "gx", shifts(n_x, 1))
    after = lax.ppermute(first, "gx", shifts(n_x, -1))
    density = call(dense_kernel, tall, [VMEM] * 2)(packed, t)
    result = call(second_kernel, tall, [VMEM] * 7)(t, packed, heat, beside, outer, before, after)
    return result, density


def solution(mesh):
    return jax.shard_map(
        local,
        mesh=mesh,
        in_specs=(
            P(None, "gx", "gy", "gz"),
            P(None, "gx", "gy", "gz"),
            P("gx", "gy", "gz"),
            P(("gx", "gy", "gz"), None),
            P("gx", ("gy", "gz"), None),
            P("gx", ("gy", "gz"), None),
        ),
        out_specs=(P("gx", ("gy", "gz"), None), P("gx", ("gy", "gz"), None)),
        check_vma=False,
    )
```

```python
import math

import jax
import jax.numpy as jnp
from jax import lax
from jax.experimental import pallas as pl
from jax.experimental.pallas import tpu as pltpu
from jax.sharding import PartitionSpec as P

ITERS = 4
W = 4
CX, CY, CZ = 16, 8, 256
TX, TY = CX // 2, CY // 2
NY = CY + 2 * W
LANES = 128
FIELDS = 8
TILES = 2 * FIELDS

eps_table = (3.0, 9.0, 12.0, 1.0)
sig_table = (0.05, 0.01, 0.4, 0.0)
courant_dt = 0.99 / math.sqrt(3.0)
loss_table = tuple(s * courant_dt / (2.0 * e) for s, e in zip(sig_table, eps_table))
ca_table = tuple((1.0 - l) / (1.0 + l) for l in loss_table)
cb_table = tuple(courant_dt / (e * (1.0 + l)) for l, e in zip(loss_table, eps_table))

F32 = jnp.float32
VMEM = pl.BlockSpec(memory_space=pltpu.VMEM)
HBM = pl.BlockSpec(memory_space=pltpu.HBM)

Y_PLANES = (4, 4, 4, 4, 3, 4, 3, 3)
Y_START = []
for planes in Y_PLANES:
    Y_START += [sum(2 * p for p in Y_PLANES[: len(Y_START) // 2]), 0]
    Y_START[-1] = Y_START[-2] + planes
Y_TOTAL = 2 * sum(Y_PLANES)


def side_rows(low):
    table, place = {}, 0
    for k in range(TILES + 1):
        field = k // 2
        most = W - 1 if field in ((3, 6, 7) if low else (3, 4, 5, 6, 7)) else W
        for j in range(NY):
            corner = W - j if low else j - (W + CY - 1)
            count = min(most, W - corner) if corner > 0 else most
            table[k, j] = (place, count)
            place += count
    return table, place


LOW_TABLE, LOW_ROWS = side_rows(True)
HIGH_TABLE, HIGH_ROWS = side_rows(False)


def f32(*shape):
    return jax.ShapeDtypeStruct(shape, F32)


def call(body, outs, ins, scratch=(), limit=24):
    return pl.pallas_call(
        body,
        out_shape=outs,
        in_specs=ins,
        out_specs=jax.tree.map(lambda _: VMEM, outs),
        scratch_shapes=list(scratch),
        compiler_params=pltpu.CompilerParams(vmem_limit_bytes=limit * 1024 * 1024),
    )


def swaps(size, first):
    pairs = [(i, i + 1) for i in range(first, size - 1, 2)]
    return pairs + [(j, i) for i, j in pairs]


def shifts(size, step):
    return [(i, i + step) for i in range(size) if 0 <= i + step < size]


def lane_ids(shape):
    return lax.broadcasted_iota(jnp.int32, shape, len(shape) - 1)


def parity():
    return lax.rem(lax.axis_index("gy"), 2)


def pack_kernel(spots_hbm, e_hbm, h_hbm, phase_hbm, t_hbm, own, out_a, out_b, shared, spots, e_ref, h_ref, phase_ref, heat, sems):
    odd = parity()
    copies = [
        pltpu.make_async_copy(spots_hbm, spots, sems.at[0]),
        pltpu.make_async_copy(phase_hbm, phase_ref, sems.at[1]),
    ]
    for c in range(3):
        copies.append(pltpu.make_async_copy(e_hbm.at[c], e_ref.at[c], sems.at[2 + c]))
    for c in range(3):
        copies.append(pltpu.make_async_copy(h_hbm.at[c], h_ref.at[c], sems.at[5 + c]))
    copies.append(pltpu.make_async_copy(t_hbm, heat, sems.at[8]))
    for copy in copies:
        copy.start()
    for t in range(2):
        own[14 + t] = jnp.zeros((CY, CX, LANES), F32)

    lane = lane_ids((1, LANES))

    def drop(i, carry):
        spot = spots[0, i]
        x, y = spot >> 11, (spot >> 8) & (CY - 1)
        t, place_z = 14 + ((spot >> 7) & 1), spot & (LANES - 1)
        row = own[t, y, pl.ds(x, 1), :]
        own[t, y, pl.ds(x, 1), :] = row + (lane == place_z).astype(F32)
        return carry

    copies[0].wait()
    lax.fori_loop(0, spots.shape[1], drop, 0)

    def spread(k, source):
        for y in range(CY):
            for t in range(2):
                own[k + t, y] = source[pl.ds(t * CY + y, CX, stride=2 * CY), :].astype(F32)

    copies[1].wait()
    phase_ref[...] += 1
    spread(12, phase_ref)
    for c in range(3):
        copies[2 + c].wait()
        spread(2 * c, e_ref.at[c])
    for c in range(3):
        copies[5 + c].wait()
        spread(2 * (3 + c), h_ref.at[c])
    for k in range(TILES):
        planes = Y_PLANES[k // 2]
        for i in range(planes):
            out_a[Y_START[k] + i] = own[k, odd * (CY - planes) + i]
            out_b[Y_START[k] + i] = own[k, (1 - odd) * (CY - planes) + i]

    wide = lane_ids((CX, LANES))
    slot = wide // 8
    for y in range(CY):
        edge = jnp.zeros((CX, LANES), F32)
        for f in range(FIELDS):
            shift = 8 * f + W
            ends = jnp.where(wide < LANES // 2, own[2 * f, y], own[2 * f + 1, y])
            edge = jnp.where(slot == f, pltpu.roll(ends, shift, 1), edge)
        shared[pl.ds(CX * y, CX), :] = edge
    copies[8].wait()
    for k in range(heat.shape[2] // LANES):
        shared[pl.ds(CX * CY + k * TX, TX), :] = heat[:, 0, pl.ds(k * LANES, LANES)]


def edge_kernel(from_below, from_above, own_z, out_a, out_b):
    odd, me = parity(), lax.axis_index("gz")
    upper = lane_ids((CX, LANES)) % 8 >= W
    has_below = (me > 0).astype(F32)
    has_above = (me < lax.axis_size("gz") - 1).astype(F32)
    for y in range(CY):
        rows = pl.ds(CX * y, CX)
        own_z[y] = jnp.where(upper, from_above[rows, :] * has_above, from_below[rows, :] * has_below)
    thermal = pl.ds(CX * CY, from_below.shape[0] - CX * CY)
    below, above = from_below[thermal, :], from_above[thermal, :]
    for out, up in ((out_a, odd), (out_b, 1 - odd)):
        for i in range(W):
            out[pl.ds(CX * i, CX), :] = own_z[up * (CY - W) + i]
        out[pl.ds(CX * W, thermal.size), :] = jnp.where(up == 1, below, above)


def moved(out, table, up, k, j, rows):
    start, count = table[k, j]
    if count:
        out[pl.ds(start, count), :] = rows[CX - count :] if up else rows[:count]


def middle_kernel(own, own_z, warmth, out_up, out_down):
    for out, table, up in ((out_up, LOW_TABLE, True), (out_down, HIGH_TABLE, False)):
        for k in range(TILES + 1):
            for y in range(CY):
                moved(out, table, up, k, W + y, own_z[y] if k == TILES else own[k, y])
    for k in range(warmth.shape[0] // TX):
        out_up[pl.ds(LOW_ROWS + k, 1), :] = warmth[pl.ds(k * TX + TX - 1, 1), :]
        out_down[pl.ds(HIGH_ROWS + k, 1), :] = warmth[pl.ds(k * TX, 1), :]


def side_kernel(mid_up, mid_down, in_a, in_b, z_a, z_b, out_up, out_down):
    odd = parity()
    out_up[...] = mid_up[...]
    out_down[...] = mid_down[...]

    def outside(low, high, z_low, z_high):
        for out, table, up in ((out_up, LOW_TABLE, True), (out_down, HIGH_TABLE, False)):
            for k in range(TILES):
                planes = Y_PLANES[k // 2]
                for i in range(planes):
                    moved(out, table, up, k, W - planes + i, low[Y_START[k] + i])
                    moved(out, table, up, k, W + CY + i, high[Y_START[k] + i])
            for i in range(W):
                moved(out, table, up, TILES, i, z_low[pl.ds(CX * i, CX), :])
                moved(out, table, up, TILES, W + CY + i, z_high[pl.ds(CX * i, CX), :])

    @pl.when(odd == 1)
    def _():
        outside(in_b, in_a, z_b, z_a)

    @pl.when(odd == 0)
    def _():
        outside(in_a, in_b, z_a, z_b)


HALF = CX // 2


def planes_of(own, own_z, in_a, in_b, z_a, z_b, put):
    for y in range(CY):
        for k in range(TILES):
            put(k, W + y, own[k, y])
        put(TILES, W + y, own_z[y])

    def outside(low, high, z_low, z_high):
        for k in range(TILES):
            planes = Y_PLANES[k // 2]
            if planes < W:
                put(k, 0, jnp.zeros((CX, LANES), F32))
                put(k, NY - 1, jnp.zeros((CX, LANES), F32))
            for i in range(planes):
                put(k, W - planes + i, low[Y_START[k] + i])
                put(k, W + CY + i, high[Y_START[k] + i])
        for i in range(W):
            put(TILES, i, z_low[pl.ds(CX * i, CX), :])
            put(TILES, W + CY + i, z_high[pl.ds(CX * i, CX), :])

    @pl.when(parity() == 1)
    def _():
        outside(in_b, in_a, z_b, z_a)

    @pl.when(parity() == 0)
    def _():
        outside(in_a, in_b, z_a, z_b)


def half_lanes(k):
    return pl.ds((k % 2) * LANES, LANES)


def leapfrog(s, zs, coef, reach, power, keep, middle):
    span = 3 * LANES
    narrow = lane_ids((CX, LANES))
    near = (narrow < W) | (narrow >= LANES - W)
    for j in range(NY):
        edges = zs[j]
        for f in range(FIELDS):
            s[f, j, :, 2 * LANES :] = jnp.where(near, pltpu.roll(edges, LANES - (8 * f + W), 1), 0.0)

    wide = lane_ids((CX, span))
    x = lax.broadcasted_iota(jnp.int32, (CX, span), 0)
    inside = jnp.full((CX, span), courant_dt, F32)
    if not middle:
        inside = jnp.where((x < W) & (lax.axis_index("gx") == 0), 0.0, inside)
    inside = jnp.where((wide >= span - W) & (lax.axis_index("gz") == 0), 0.0, inside)
    reach[0] = inside
    reach[1] = inside * (lax.axis_index("gy") > 0).astype(F32)

    def coefs(j, carry):
        phase = s[6, j]

        def chosen(table):
            value = jnp.zeros_like(phase)
            for index in range(4):
                value = jnp.where(phase == index + 1.0, table[index], value)
            return value

        coef[0, j] = chosen(ca_table)
        coef[1, j] = chosen(cb_table)
        coef[2, j] = chosen(sig_table)
        return carry

    lax.fori_loop(0, NY, coefs, 0)

    for step in range(ITERS):
        wave = 60.0 * math.sin(0.6 * (step + 0.5) * courant_dt)

        def ahead_x(value, q, j):
            turned = pltpu.roll(value, CX - 1, 0)
            if middle:
                keep[step, q, pl.ds(j, 1), :] = value[W : W + 1]
                return turned
            return jnp.where(x == HALF - 1, keep[step, q, pl.ds(j, 1), :], turned)

        def behind_x(value, q, j, cells):
            turned = pltpu.roll(value, 1, 0)
            if middle:
                keep[step, q, pl.ds(j, 1), cells] = value[CX - W - 1 : CX - W]
                return turned
            return jnp.where(x[:, cells] == HALF, keep[step, q, pl.ds(j, 1), cells], turned)

        def magnetic(j):
            ex, ey, ez = s[0, j], s[1, j], s[2, j]
            step_h = reach[0 if j >= W else 1]
            s[3, j] -= step_h * ((s[2, j + 1] - ez) - (pltpu.roll(ey, span - 1, 1) - ey))
            s[4, j] -= step_h * ((pltpu.roll(ex, span - 1, 1) - ex) - (ahead_x(ez, 1, j) - ez))
            s[5, j] -= step_h * ((ahead_x(ey, 0, j) - ey) - (s[0, j + 1] - ex))

        def electric(j):
            hx, hy, hz = s[3, j], s[4, j], s[5, j]
            cells = slice(0, 2 * LANES if step == ITERS - 1 else span)
            ca, cb, sig = coef[0, j, :, cells], coef[1, j, :, cells], coef[2, j, :, cells]
            hy_z, hx_z = pltpu.roll(hy, 1, 1)[:, cells], pltpu.roll(hx, 1, 1)[:, cells]
            hx, hy, hz = hx[:, cells], hy[:, cells], hz[:, cells]
            hx_y, hz_y = s[3, j - 1, :, cells], s[5, j - 1, :, cells]
            ex = ca * s[0, j, :, cells] + cb * ((hz - hz_y) - (hy - hy_z))
            ey = ca * s[1, j, :, cells] + cb * ((hx - hx_z) - (hz - behind_x(hz, 3, j, cells)))
            curl = (hy - behind_x(hy, 2, j, cells)) - (hx - hx_y)
            ez = ca * s[2, j, :, cells] + cb * (curl - s[7, j, :, cells] * wave)
            if step < ITERS - 1:
                s[0, j] = ex
                s[1, j] = ey
                s[2, j] = ez
            p = j - W
            if 0 <= p < CY:
                own = slice(0, 2 * LANES)
                ex, ey, ez = ex[:, own], ey[:, own], ez[:, own]
                now = sig[:, own] * (ex * ex + ey * ey + ez * ez)
                power[p] = now if step == 0 else power[p] + now

        magnetic(step)
        for j in range(step + 1, NY - 1 - step):
            magnetic(j)
            electric(j)


def middle_field_kernel(own, own_z, in_a, in_b, z_a, z_b, power, keep, s, zs, coef, reach):
    def put(k, j, rows):
        if k == TILES:
            zs[j] = rows
        else:
            s[k // 2, j, :, half_lanes(k)] = rows

    planes_of(own, own_z, in_a, in_b, z_a, z_b, put)
    leapfrog(s, zs, coef, reach, power, keep, True)


def field_kernel(own, own_z, in_a, in_b, z_a, z_b, from_low, from_high, base, inner, keep, out, s, zs, coef, reach, power, pair):
    def store(k, j, start, rows):
        here = pl.ds(start, rows.shape[0])
        if k == TILES:
            zs[j, here, :] = rows
        else:
            s[k // 2, j, here, half_lanes(k)] = rows

    for j in range(NY):
        for k in range(TILES + 1):
            for message, table, edge in ((from_low, LOW_TABLE, 0), (from_high, HIGH_TABLE, CX - W)):
                start, count = table[k, j]
                if count < W:
                    store(k, j, edge, jnp.zeros((W, LANES), F32))
                if count:
                    store(k, j, W - count if edge == 0 else edge, message[pl.ds(start, count), :])

    def put(k, j, rows):
        store(k, j, W, rows[:W])
        store(k, j, HALF, rows[CX - W :])

    planes_of(own, own_z, in_a, in_b, z_a, z_b, put)
    leapfrog(s, zs, coef, reach, power, keep, False)

    rows = []
    for t in range(TY):
        halves = []
        for k in range(2):
            lanes = half_lanes(k)
            ends = power[2 * t, :, lanes] + power[2 * t + 1, :, lanes]
            centre = inner[2 * t, :, lanes] + inner[2 * t + 1, :, lanes]
            pair[pl.ds(0, W), :] = ends[W : 2 * W]
            pair[pl.ds(W, HALF), :] = centre[W : W + HALF]
            pair[pl.ds(W + HALF, W), :] = ends[HALF : HALF + W]
            halves.append(pair[pl.ds(0, TX, stride=2), :] + pair[pl.ds(1, TX, stride=2), :])
        rows.append(jnp.concatenate(halves, axis=1))
    stacked = jnp.concatenate(rows, axis=0)
    source = lax.broadcasted_iota(jnp.int32, (2 * LANES, LANES), 0)
    target = lax.broadcasted_iota(jnp.int32, (2 * LANES, LANES), 1)
    gather = (source // 2 == target).astype(F32)
    summed = jnp.dot(stacked, gather, precision=lax.Precision.HIGHEST, preferred_element_type=F32)
    summed = summed * (1.0 / (8.0 * ITERS))
    for d in range(TY):
        for i, t in enumerate((d - 1, d, d + 1)):
            out[d, i] = summed[TX * t : TX * (t + 1)] if 0 <= t < TY else jnp.zeros((TX, LANES), F32)
        for k in range(base.shape[1] // LANES):
            out[d, 3 + k] = base[:, pl.ds(k * LANES, LANES)]


def beside_z(t):
    wide = lane_ids(t.shape)
    span = t.shape[1]
    ahead = jnp.where(wide == span - 1, 0.0, pltpu.roll(t, span - 1, 1))
    behind = jnp.where(wide == 0, 0.0, pltpu.roll(t, 1, 1))
    return ahead + behind


def beside_x(t, before, after):
    rows = t.shape[0]
    x = lax.broadcasted_iota(jnp.int32, t.shape, 0)
    ahead = jnp.where(x == rows - 1, after, pltpu.roll(t, rows - 1, 0))
    behind = jnp.where(x == 0, before, pltpu.roll(t, 1, 0))
    return ahead + behind


def densified(packing, warmth):
    return packing + 0.3 * (1.0 - packing) * jnp.exp(-3.0 / (1.0 + warmth))


def warm_kernel(warmth, packing, from_below, from_above, z_a, z_b, from_low, from_high, base, packed):
    odd, me = parity(), lax.axis_index("gz")
    tiles = packing.shape[2] // LANES
    t, p, sides, before, after = [], [], [], [], []
    for k in range(tiles):
        near, far = pl.ds(CX * CY + k * TX, TX), pl.ds(CX * W + k * TX, TX)
        low = jnp.where(odd == 1, z_b[far, :], z_a[far, :])
        high = jnp.where(odd == 1, z_a[far, :], z_b[far, :])
        low = jnp.where(me == 0, low, from_below[near, :])
        high = jnp.where(me == lax.axis_size("gz") - 1, high, from_above[near, :])
        sides.append(low + high)
        before.append(from_low[pl.ds(LOW_ROWS + k, 1), :])
        after.append(from_high[pl.ds(HIGH_ROWS + k, 1), :])
        t.append(warmth[pl.ds(k * TX, TX), :])
        p.append(packing[:, 0, pl.ds(k * LANES, LANES)])
    t, p, sides, before, after = (jnp.concatenate(parts, axis=1) for parts in (t, p, sides, before, after))
    lap = beside_x(t, before, after) + sides + beside_z(t) - 6.0 * t
    base[...] = t + 0.1 * ((0.2 + p) * lap)
    packed[...] = densified(p, t)


def first_kernel(base, heat, warmth, beside, first, last):
    me = lax.axis_index("gz")
    tiles = heat.shape[0]
    has_low = (me > 0).astype(F32)
    has_high = (me < tiles - 1).astype(F32)
    low, high = jnp.maximum(me - 1, 0), jnp.minimum(me + 1, tiles - 1)
    for k in range(tiles):
        lanes = pl.ds(k * LANES, LANES)
        t = base[:, lanes] + heat[k, 1]
        warmth[:, lanes] = t
        first[:, lanes] = t[:1]
        last[:, lanes] = t[TX - 1 :]
        below = (heat[low, 3 + k] + heat[k, 0]) * has_low
        above = (heat[high, 3 + k] + heat[k, 2]) * has_high
        beside[:, lanes] = below + above


def dense_kernel(packed, warmth, density):
    dense = densified(packed[...], warmth[...])
    for k in range(dense.shape[1] // LANES):
        here = slice(k * LANES, (k + 1) * LANES)
        density[:, 0, here] = dense[:, here]


def second_kernel(warmth, packed, heat, beside, across, before, after, out):
    t = warmth[...]
    lap = beside_x(t, before[...], after[...]) + beside[...] + across[...] + beside_z(t) - 6.0 * t
    grown = t + 0.1 * ((0.2 + packed[...]) * lap)
    for k in range(heat.shape[0]):
        here = slice(k * LANES, (k + 1) * LANES)
        out[:, 0, here] = grown[:, here] + heat[k, 1]


def tile_rows(a):
    lead = a.shape[:-3]
    a = a.reshape(lead + (CX, CY, 2, LANES))
    return jnp.swapaxes(a, -3, -2).reshape(lead + (2 * CX * CY, LANES))


def local(e, h, phase, spots, warmth, packing):
    n_y, n_z, n_x = lax.axis_size("gy"), lax.axis_size("gz"), lax.axis_size("gx")
    across, within = swaps(n_y, 1), swaps(n_y, 0)
    span = warmth.shape[2]
    pencil_rows = TX * span // LANES

    own, to_a, to_b, shared = call(
        pack_kernel,
        (f32(TILES, CY, CX, LANES), f32(Y_TOTAL, CX, LANES), f32(Y_TOTAL, CX, LANES), f32(CX * CY + pencil_rows, LANES)),
        [HBM] * 5,
        scratch=[
            pltpu.SMEM(spots.shape, jnp.int32),
            pltpu.VMEM((3, 2 * CX * CY, LANES), F32),
            pltpu.VMEM((3, 2 * CX * CY, LANES), F32),
            pltpu.VMEM((2 * CX * CY, LANES), jnp.int32),
            pltpu.VMEM(warmth.shape, F32),
            pltpu.SemaphoreType.DMA((9,)),
        ],
        limit=60,
    )(spots, tile_rows(e), tile_rows(h), tile_rows(phase), warmth)
    in_a = lax.ppermute(to_a, "gy", across)
    in_b = lax.ppermute(to_b, "gy", within)
    from_below = lax.ppermute(shared, "gz", [(i, (i + 1) % n_z) for i in range(n_z)])
    from_above = lax.ppermute(shared, "gz", [(i, (i - 1) % n_z) for i in range(n_z)])
    edge = f32(CX * W + pencil_rows, LANES)
    own_z, z_a, z_b = call(edge_kernel, (f32(CY, CX, LANES), edge, edge), [VMEM] * 2)(from_below, from_above)
    z_a = lax.ppermute(z_a, "gy", across)
    z_b = lax.ppermute(z_b, "gy", within)

    def block(rows):
        rows += span // LANES
        return f32(rows + (-rows) % 8, LANES)

    pencil_tiles = shared[CX * CY :]
    blocks = (block(LOW_ROWS), block(HIGH_ROWS))
    middle = call(middle_kernel, blocks, [VMEM] * 3)(own, own_z, pencil_tiles)
    to_up, to_down = call(side_kernel, blocks, [VMEM] * 6)(*middle, in_a, in_b, z_a, z_b)
    from_low = lax.ppermute(to_up, "gx", shifts(n_x, 1))
    from_high = lax.ppermute(to_down, "gx", shifts(n_x, -1))
    pencil, tall, line = f32(TX, span), f32(TX, 1, span), f32(1, span)
    base, packed = call(warm_kernel, (pencil, pencil), [VMEM] * 8)(
        pencil_tiles, packing, from_below, from_above, z_a, z_b, from_low, from_high
    )
    work = [
        pltpu.VMEM((FIELDS, NY, CX, 3 * LANES), F32),
        pltpu.VMEM((NY, CX, LANES), F32),
        pltpu.VMEM((3, NY, CX, 3 * LANES), F32),
        pltpu.VMEM((2, CX, 3 * LANES), F32),
    ]
    power = (CY, CX, 2 * LANES)
    local_parts = (own, own_z, in_a, in_b, z_a, z_b)
    inner = call(middle_field_kernel, (f32(*power), f32(ITERS, 4, NY, 3 * LANES)), [VMEM] * 6, scratch=work)(*local_parts)
    heat = call(
        field_kernel,
        f32(TY, 3 + span // LANES, TX, LANES),
        [VMEM] * 11,
        scratch=work + [pltpu.VMEM(power, F32), pltpu.VMEM((CX, LANES), F32)],
    )(*local_parts, from_low, from_high, base, *inner)
    heat = lax.all_to_all(heat, "gz", split_axis=0, concat_axis=0, tiled=True)
    t, beside, first, last = call(first_kernel, (pencil, pencil, line, line), [VMEM] * 2)(base, heat)
    ends = [(i, i + 1) for i in range(n_z - 1, n_y * n_z - 1, n_z)]
    outer = lax.ppermute(t, ("gy", "gz"), ends + [(j, i) for i, j in ends])
    before = lax.ppermute(last, "gx", shifts(n_x, 1))
    after = lax.ppermute(first, "gx", shifts(n_x, -1))
    density = call(dense_kernel, tall, [VMEM] * 2)(packed, t)
    result = call(second_kernel, tall, [VMEM] * 7)(t, packed, heat, beside, outer, before, after)
    return result, density


def solution(mesh):
    return jax.shard_map(
        local,
        mesh=mesh,
        in_specs=(
            P(None, "gx", "gy", "gz"),
            P(None, "gx", "gy", "gz"),
            P("gx", "gy", "gz"),
            P(("gx", "gy", "gz"), None),
            P("gx", ("gy", "gz"), None),
            P("gx", ("gy", "gz"), None),
        ),
        out_specs=(P("gx", ("gy", "gz"), None), P("gx", ("gy", "gz"), None)),
        check_vma=False,
    )
```

```python
import math

import jax
import jax.numpy as jnp
from jax import lax
from jax.experimental import pallas as pl
from jax.experimental.pallas import tpu as pltpu
from jax.sharding import PartitionSpec as P

ITERS = 4
W = 4
CX, CY, CZ = 16, 8, 256
TX, TY = CX // 2, CY // 2
NY = CY + 2 * W
LANES = 128
FIELDS = 8
TILES = 2 * FIELDS

eps_table = (3.0, 9.0, 12.0, 1.0)
sig_table = (0.05, 0.01, 0.4, 0.0)
courant_dt = 0.99 / math.sqrt(3.0)
loss_table = tuple(s * courant_dt / (2.0 * e) for s, e in zip(sig_table, eps_table))
ca_table = tuple((1.0 - l) / (1.0 + l) for l in loss_table)
cb_table = tuple(courant_dt / (e * (1.0 + l)) for l, e in zip(loss_table, eps_table))

F32 = jnp.float32
VMEM = pl.BlockSpec(memory_space=pltpu.VMEM)
HBM = pl.BlockSpec(memory_space=pltpu.HBM)

Y_PLANES = (4, 4, 4, 4, 3, 4, 3, 3)
Y_START = []
for planes in Y_PLANES:
    Y_START += [sum(2 * p for p in Y_PLANES[: len(Y_START) // 2]), 0]
    Y_START[-1] = Y_START[-2] + planes
Y_TOTAL = 2 * sum(Y_PLANES)


def side_rows(low):
    table, place = {}, 0
    for k in range(TILES + 1):
        field = k // 2
        most = W - 1 if field in ((3, 6, 7) if low else (3, 4, 5, 6, 7)) else W
        for j in range(NY):
            corner = W - j if low else j - (W + CY - 1)
            count = min(most, W - corner) if corner > 0 else most
            table[k, j] = (place, count)
            place += count
    return table, place


LOW_TABLE, LOW_ROWS = side_rows(True)
HIGH_TABLE, HIGH_ROWS = side_rows(False)


def f32(*shape):
    return jax.ShapeDtypeStruct(shape, F32)


def call(body, outs, ins, scratch=(), limit=24):
    return pl.pallas_call(
        body,
        out_shape=outs,
        in_specs=ins,
        out_specs=jax.tree.map(lambda _: VMEM, outs),
        scratch_shapes=list(scratch),
        compiler_params=pltpu.CompilerParams(vmem_limit_bytes=limit * 1024 * 1024),
    )


def swaps(size, first):
    pairs = [(i, i + 1) for i in range(first, size - 1, 2)]
    return pairs + [(j, i) for i, j in pairs]


def shifts(size, step):
    return [(i, i + step) for i in range(size) if 0 <= i + step < size]


def lane_ids(shape):
    return lax.broadcasted_iota(jnp.int32, shape, len(shape) - 1)


def parity():
    return lax.rem(lax.axis_index("gy"), 2)


def pack_kernel(spots_hbm, e_hbm, h_hbm, phase_hbm, t_hbm, own, out_a, out_b, shared, spots, e_ref, h_ref, phase_ref, heat, sems):
    odd = parity()
    copies = [
        pltpu.make_async_copy(spots_hbm, spots, sems.at[0]),
        pltpu.make_async_copy(phase_hbm, phase_ref, sems.at[1]),
    ]
    for c in range(3):
        copies.append(pltpu.make_async_copy(e_hbm.at[c], e_ref.at[c], sems.at[2 + c]))
    for c in range(3):
        copies.append(pltpu.make_async_copy(h_hbm.at[c], h_ref.at[c], sems.at[5 + c]))
    copies.append(pltpu.make_async_copy(t_hbm, heat, sems.at[8]))
    for copy in copies:
        copy.start()
    for t in range(2):
        own[14 + t] = jnp.zeros((CY, CX, LANES), F32)

    lane = lane_ids((1, LANES))

    def drop(i, carry):
        spot = spots[0, i]
        x, y = spot >> 11, (spot >> 8) & (CY - 1)
        t, place_z = 14 + ((spot >> 7) & 1), spot & (LANES - 1)
        row = own[t, y, pl.ds(x, 1), :]
        own[t, y, pl.ds(x, 1), :] = row + (lane == place_z).astype(F32)
        return carry

    copies[0].wait()
    lax.fori_loop(0, spots.shape[1], drop, 0)

    def spread(k, source):
        for y in range(CY):
            for t in range(2):
                own[k + t, y] = source[pl.ds(t * CY + y, CX, stride=2 * CY), :].astype(F32)

    copies[1].wait()
    phase_ref[...] += 1
    spread(12, phase_ref)
    for c in range(3):
        copies[2 + c].wait()
        spread(2 * c, e_ref.at[c])
    for c in range(3):
        copies[5 + c].wait()
        spread(2 * (3 + c), h_ref.at[c])
    for k in range(TILES):
        planes = Y_PLANES[k // 2]
        for i in range(planes):
            out_a[Y_START[k] + i] = own[k, odd * (CY - planes) + i]
            out_b[Y_START[k] + i] = own[k, (1 - odd) * (CY - planes) + i]

    wide = lane_ids((CX, LANES))
    slot = wide // 8
    for y in range(CY):
        edge = jnp.zeros((CX, LANES), F32)
        for f in range(FIELDS):
            shift = 8 * f + W
            ends = jnp.where(wide < LANES // 2, own[2 * f, y], own[2 * f + 1, y])
            edge = jnp.where(slot == f, pltpu.roll(ends, shift, 1), edge)
        shared[pl.ds(CX * y, CX), :] = edge
    copies[8].wait()
    for k in range(heat.shape[2] // LANES):
        shared[pl.ds(CX * CY + k * TX, TX), :] = heat[:, 0, pl.ds(k * LANES, LANES)]


def edge_kernel(from_below, from_above, own_z, out_a, out_b):
    odd, me = parity(), lax.axis_index("gz")
    upper = lane_ids((CX, LANES)) % 8 >= W
    has_below = (me > 0).astype(F32)
    has_above = (me < lax.axis_size("gz") - 1).astype(F32)
    for y in range(CY):
        rows = pl.ds(CX * y, CX)
        own_z[y] = jnp.where(upper, from_above[rows, :] * has_above, from_below[rows, :] * has_below)
    thermal = pl.ds(CX * CY, from_below.shape[0] - CX * CY)
    below, above = from_below[thermal, :], from_above[thermal, :]
    for out, up in ((out_a, odd), (out_b, 1 - odd)):
        for i in range(W):
            out[pl.ds(CX * i, CX), :] = own_z[up * (CY - W) + i]
        out[pl.ds(CX * W, thermal.size), :] = jnp.where(up == 1, below, above)


def moved(out, table, up, k, j, rows):
    start, count = table[k, j]
    if count:
        out[pl.ds(start, count), :] = rows[CX - count :] if up else rows[:count]


def middle_kernel(own, own_z, warmth, out_up, out_down):
    for out, table, up in ((out_up, LOW_TABLE, True), (out_down, HIGH_TABLE, False)):
        for k in range(TILES + 1):
            for y in range(CY):
                moved(out, table, up, k, W + y, own_z[y] if k == TILES else own[k, y])
    for k in range(warmth.shape[0] // TX):
        out_up[pl.ds(LOW_ROWS + k, 1), :] = warmth[pl.ds(k * TX + TX - 1, 1), :]
        out_down[pl.ds(HIGH_ROWS + k, 1), :] = warmth[pl.ds(k * TX, 1), :]


def side_kernel(mid_up, mid_down, in_a, in_b, z_a, z_b, out_up, out_down):
    odd = parity()
    out_up[...] = mid_up[...]
    out_down[...] = mid_down[...]

    def outside(low, high, z_low, z_high):
        for out, table, up in ((out_up, LOW_TABLE, True), (out_down, HIGH_TABLE, False)):
            for k in range(TILES):
                planes = Y_PLANES[k // 2]
                for i in range(planes):
                    moved(out, table, up, k, W - planes + i, low[Y_START[k] + i])
                    moved(out, table, up, k, W + CY + i, high[Y_START[k] + i])
            for i in range(W):
                moved(out, table, up, TILES, i, z_low[pl.ds(CX * i, CX), :])
                moved(out, table, up, TILES, W + CY + i, z_high[pl.ds(CX * i, CX), :])

    @pl.when(odd == 1)
    def _():
        outside(in_b, in_a, z_b, z_a)

    @pl.when(odd == 0)
    def _():
        outside(in_a, in_b, z_a, z_b)


HALF = CX // 2


def planes_of(own, own_z, in_a, in_b, z_a, z_b, put):
    for y in range(CY):
        for k in range(TILES):
            put(k, W + y, own[k, y])
        put(TILES, W + y, own_z[y])

    def outside(low, high, z_low, z_high):
        for k in range(TILES):
            planes = Y_PLANES[k // 2]
            if planes < W:
                put(k, 0, jnp.zeros((CX, LANES), F32))
                put(k, NY - 1, jnp.zeros((CX, LANES), F32))
            for i in range(planes):
                put(k, W - planes + i, low[Y_START[k] + i])
                put(k, W + CY + i, high[Y_START[k] + i])
        for i in range(W):
            put(TILES, i, z_low[pl.ds(CX * i, CX), :])
            put(TILES, W + CY + i, z_high[pl.ds(CX * i, CX), :])

    @pl.when(parity() == 1)
    def _():
        outside(in_b, in_a, z_b, z_a)

    @pl.when(parity() == 0)
    def _():
        outside(in_a, in_b, z_a, z_b)


def half_lanes(k):
    return pl.ds((k % 2) * LANES, LANES)


def leapfrog(s, zs, coef, reach, power, keep, middle):
    span = 3 * LANES
    narrow = lane_ids((CX, LANES))
    near = (narrow < W) | (narrow >= LANES - W)
    for j in range(NY):
        edges = zs[j]
        for f in range(FIELDS):
            s[f, j, :, 2 * LANES :] = jnp.where(near, pltpu.roll(edges, LANES - (8 * f + W), 1), 0.0)

    wide = lane_ids((CX, span))
    x = lax.broadcasted_iota(jnp.int32, (CX, span), 0)
    inside = jnp.full((CX, span), courant_dt, F32)
    if not middle:
        inside = jnp.where((x < W) & (lax.axis_index("gx") == 0), 0.0, inside)
    inside = jnp.where((wide >= span - W) & (lax.axis_index("gz") == 0), 0.0, inside)
    reach[0] = inside
    reach[1] = inside * (lax.axis_index("gy") > 0).astype(F32)

    for j in range(NY):
        phase = s[6, j]
        for i, table in enumerate((ca_table, cb_table, sig_table)):
            if i == 2 and not W <= j < W + CY:
                continue
            value = jnp.zeros_like(phase)
            for index in range(4):
                if table[index]:
                    value = jnp.where(phase == index + 1.0, table[index], value)
            coef[i, j] = value

    for step in range(ITERS):
        wave = 60.0 * math.sin(0.6 * (step + 0.5) * courant_dt)

        def ahead_x(value, q, j):
            turned = pltpu.roll(value, CX - 1, 0)
            if middle:
                keep[step, q, pl.ds(j, 1), :] = value[W : W + 1]
                return turned
            return jnp.where(x == HALF - 1, keep[step, q, pl.ds(j, 1), :], turned)

        def behind_x(value, q, j, cells):
            turned = pltpu.roll(value, 1, 0)
            if middle:
                keep[step, q, pl.ds(j, 1), cells] = value[CX - W - 1 : CX - W]
                return turned
            return jnp.where(x[:, cells] == HALF, keep[step, q, pl.ds(j, 1), cells], turned)

        def magnetic(j):
            ex, ey, ez = s[0, j], s[1, j], s[2, j]
            step_h = reach[0 if j >= W else 1]
            s[3, j] -= step_h * ((s[2, j + 1] - ez) - (pltpu.roll(ey, span - 1, 1) - ey))
            s[4, j] -= step_h * ((pltpu.roll(ex, span - 1, 1) - ex) - (ahead_x(ez, 1, j) - ez))
            s[5, j] -= step_h * ((ahead_x(ey, 0, j) - ey) - (s[0, j + 1] - ex))

        def electric(j):
            hx, hy, hz = s[3, j], s[4, j], s[5, j]
            cells = slice(0, 2 * LANES if step == ITERS - 1 else span)
            ca, cb = coef[0, j, :, cells], coef[1, j, :, cells]
            hy_z, hx_z = pltpu.roll(hy, 1, 1)[:, cells], pltpu.roll(hx, 1, 1)[:, cells]
            hx, hy, hz = hx[:, cells], hy[:, cells], hz[:, cells]
            hx_y, hz_y = s[3, j - 1, :, cells], s[5, j - 1, :, cells]
            ex = ca * s[0, j, :, cells] + cb * ((hz - hz_y) - (hy - hy_z))
            ey = ca * s[1, j, :, cells] + cb * ((hx - hx_z) - (hz - behind_x(hz, 3, j, cells)))
            curl = (hy - behind_x(hy, 2, j, cells)) - (hx - hx_y)
            ez = ca * s[2, j, :, cells] + cb * (curl - s[7, j, :, cells] * wave)
            if step < ITERS - 1:
                s[0, j] = ex
                s[1, j] = ey
                s[2, j] = ez
            p = j - W
            if 0 <= p < CY:
                own = slice(0, 2 * LANES)
                ex, ey, ez = ex[:, own], ey[:, own], ez[:, own]
                now = coef[2, j, :, own] * (ex * ex + ey * ey + ez * ez)
                power[p] = now if step == 0 else power[p] + now

        magnetic(step)
        for j in range(step + 1, NY - 1 - step):
            magnetic(j)
            electric(j)


def middle_field_kernel(own, own_z, in_a, in_b, z_a, z_b, power, keep, s, zs, coef, reach):
    def put(k, j, rows):
        if k == TILES:
            zs[j] = rows
        else:
            s[k // 2, j, :, half_lanes(k)] = rows

    planes_of(own, own_z, in_a, in_b, z_a, z_b, put)
    leapfrog(s, zs, coef, reach, power, keep, True)


def field_kernel(own, own_z, in_a, in_b, z_a, z_b, from_low, from_high, base, inner, keep, out, s, zs, coef, reach, power, pair):
    def store(k, j, start, rows):
        here = pl.ds(start, rows.shape[0])
        if k == TILES:
            zs[j, here, :] = rows
        else:
            s[k // 2, j, here, half_lanes(k)] = rows

    for j in range(NY):
        for k in range(TILES + 1):
            for message, table, edge in ((from_low, LOW_TABLE, 0), (from_high, HIGH_TABLE, CX - W)):
                start, count = table[k, j]
                if count < W:
                    store(k, j, edge, jnp.zeros((W, LANES), F32))
                if count:
                    store(k, j, W - count if edge == 0 else edge, message[pl.ds(start, count), :])

    def put(k, j, rows):
        store(k, j, W, rows[:W])
        store(k, j, HALF, rows[CX - W :])

    planes_of(own, own_z, in_a, in_b, z_a, z_b, put)
    leapfrog(s, zs, coef, reach, power, keep, False)

    rows = []
    for t in range(TY):
        halves = []
        for k in range(2):
            lanes = half_lanes(k)
            ends = power[2 * t, :, lanes] + power[2 * t + 1, :, lanes]
            centre = inner[2 * t, :, lanes] + inner[2 * t + 1, :, lanes]
            pair[pl.ds(0, W), :] = ends[W : 2 * W]
            pair[pl.ds(W, HALF), :] = centre[W : W + HALF]
            pair[pl.ds(W + HALF, W), :] = ends[HALF : HALF + W]
            halves.append(pair[pl.ds(0, TX, stride=2), :] + pair[pl.ds(1, TX, stride=2), :])
        rows.append(jnp.concatenate(halves, axis=1))
    stacked = jnp.concatenate(rows, axis=0)
    source = lax.broadcasted_iota(jnp.int32, (2 * LANES, LANES), 0)
    target = lax.broadcasted_iota(jnp.int32, (2 * LANES, LANES), 1)
    gather = (source // 2 == target).astype(F32)
    summed = jnp.dot(stacked, gather, precision=lax.Precision.HIGHEST, preferred_element_type=F32)
    summed = summed * (1.0 / (8.0 * ITERS))
    for d in range(TY):
        for i, t in enumerate((d - 1, d, d + 1)):
            out[d, i] = summed[TX * t : TX * (t + 1)] if 0 <= t < TY else jnp.zeros((TX, LANES), F32)
        for k in range(base.shape[1] // LANES):
            out[d, 3 + k] = base[:, pl.ds(k * LANES, LANES)]


def beside_z(t):
    wide = lane_ids(t.shape)
    span = t.shape[1]
    ahead = jnp.where(wide == span - 1, 0.0, pltpu.roll(t, span - 1, 1))
    behind = jnp.where(wide == 0, 0.0, pltpu.roll(t, 1, 1))
    return ahead + behind


def beside_x(t, before, after):
    rows = t.shape[0]
    x = lax.broadcasted_iota(jnp.int32, t.shape, 0)
    ahead = jnp.where(x == rows - 1, after, pltpu.roll(t, rows - 1, 0))
    behind = jnp.where(x == 0, before, pltpu.roll(t, 1, 0))
    return ahead + behind


def densified(packing, warmth):
    return packing + 0.3 * (1.0 - packing) * jnp.exp(-3.0 / (1.0 + warmth))


def warm_kernel(warmth, packing, from_below, from_above, z_a, z_b, from_low, from_high, base, packed):
    odd, me = parity(), lax.axis_index("gz")
    tiles = packing.shape[2] // LANES
    t, p, sides, before, after = [], [], [], [], []
    for k in range(tiles):
        near, far = pl.ds(CX * CY + k * TX, TX), pl.ds(CX * W + k * TX, TX)
        low = jnp.where(odd == 1, z_b[far, :], z_a[far, :])
        high = jnp.where(odd == 1, z_a[far, :], z_b[far, :])
        low = jnp.where(me == 0, low, from_below[near, :])
        high = jnp.where(me == lax.axis_size("gz") - 1, high, from_above[near, :])
        sides.append(low + high)
        before.append(from_low[pl.ds(LOW_ROWS + k, 1), :])
        after.append(from_high[pl.ds(HIGH_ROWS + k, 1), :])
        t.append(warmth[pl.ds(k * TX, TX), :])
        p.append(packing[:, 0, pl.ds(k * LANES, LANES)])
    t, p, sides, before, after = (jnp.concatenate(parts, axis=1) for parts in (t, p, sides, before, after))
    lap = beside_x(t, before, after) + sides + beside_z(t) - 6.0 * t
    base[...] = t + 0.1 * ((0.2 + p) * lap)
    packed[...] = densified(p, t)


def first_kernel(base, heat, warmth, beside, first, last):
    me = lax.axis_index("gz")
    tiles = heat.shape[0]
    has_low = (me > 0).astype(F32)
    has_high = (me < tiles - 1).astype(F32)
    low, high = jnp.maximum(me - 1, 0), jnp.minimum(me + 1, tiles - 1)
    for k in range(tiles):
        lanes = pl.ds(k * LANES, LANES)
        t = base[:, lanes] + heat[k, 1]
        warmth[:, lanes] = t
        first[:, lanes] = t[:1]
        last[:, lanes] = t[TX - 1 :]
        below = (heat[low, 3 + k] + heat[k, 0]) * has_low
        above = (heat[high, 3 + k] + heat[k, 2]) * has_high
        beside[:, lanes] = below + above


def dense_kernel(packed, warmth, density):
    dense = densified(packed[...], warmth[...])
    for k in range(dense.shape[1] // LANES):
        here = slice(k * LANES, (k + 1) * LANES)
        density[:, 0, here] = dense[:, here]


def second_kernel(warmth, packed, heat, beside, across, before, after, out):
    t = warmth[...]
    lap = beside_x(t, before[...], after[...]) + beside[...] + across[...] + beside_z(t) - 6.0 * t
    grown = t + 0.1 * ((0.2 + packed[...]) * lap)
    for k in range(heat.shape[0]):
        here = slice(k * LANES, (k + 1) * LANES)
        out[:, 0, here] = grown[:, here] + heat[k, 1]


def tile_rows(a):
    lead = a.shape[:-3]
    a = a.reshape(lead + (CX, CY, 2, LANES))
    return jnp.swapaxes(a, -3, -2).reshape(lead + (2 * CX * CY, LANES))


def local(e, h, phase, spots, warmth, packing):
    n_y, n_z, n_x = lax.axis_size("gy"), lax.axis_size("gz"), lax.axis_size("gx")
    across, within = swaps(n_y, 1), swaps(n_y, 0)
    span = warmth.shape[2]
    pencil_rows = TX * span // LANES

    own, to_a, to_b, shared = call(
        pack_kernel,
        (f32(TILES, CY, CX, LANES), f32(Y_TOTAL, CX, LANES), f32(Y_TOTAL, CX, LANES), f32(CX * CY + pencil_rows, LANES)),
        [HBM] * 5,
        scratch=[
            pltpu.SMEM(spots.shape, jnp.int32),
            pltpu.VMEM((3, 2 * CX * CY, LANES), F32),
            pltpu.VMEM((3, 2 * CX * CY, LANES), F32),
            pltpu.VMEM((2 * CX * CY, LANES), jnp.int32),
            pltpu.VMEM(warmth.shape, F32),
            pltpu.SemaphoreType.DMA((9,)),
        ],
        limit=60,
    )(spots, tile_rows(e), tile_rows(h), tile_rows(phase), warmth)
    in_a = lax.ppermute(to_a, "gy", across)
    in_b = lax.ppermute(to_b, "gy", within)
    from_below = lax.ppermute(shared, "gz", [(i, (i + 1) % n_z) for i in range(n_z)])
    from_above = lax.ppermute(shared, "gz", [(i, (i - 1) % n_z) for i in range(n_z)])
    edge = f32(CX * W + pencil_rows, LANES)
    own_z, z_a, z_b = call(edge_kernel, (f32(CY, CX, LANES), edge, edge), [VMEM] * 2)(from_below, from_above)
    z_a = lax.ppermute(z_a, "gy", across)
    z_b = lax.ppermute(z_b, "gy", within)

    def block(rows):
        rows += span // LANES
        return f32(rows + (-rows) % 8, LANES)

    pencil_tiles = shared[CX * CY :]
    blocks = (block(LOW_ROWS), block(HIGH_ROWS))
    middle = call(middle_kernel, blocks, [VMEM] * 3)(own, own_z, pencil_tiles)
    to_up, to_down = call(side_kernel, blocks, [VMEM] * 6)(*middle, in_a, in_b, z_a, z_b)
    from_low = lax.ppermute(to_up, "gx", shifts(n_x, 1))
    from_high = lax.ppermute(to_down, "gx", shifts(n_x, -1))
    pencil, tall, line = f32(TX, span), f32(TX, 1, span), f32(1, span)
    base, packed = call(warm_kernel, (pencil, pencil), [VMEM] * 8)(
        pencil_tiles, packing, from_below, from_above, z_a, z_b, from_low, from_high
    )
    work = [
        pltpu.VMEM((FIELDS, NY, CX, 3 * LANES), F32),
        pltpu.VMEM((NY, CX, LANES), F32),
        pltpu.VMEM((3, NY, CX, 3 * LANES), F32),
        pltpu.VMEM((2, CX, 3 * LANES), F32),
    ]
    power = (CY, CX, 2 * LANES)
    local_parts = (own, own_z, in_a, in_b, z_a, z_b)
    inner = call(middle_field_kernel, (f32(*power), f32(ITERS, 4, NY, 3 * LANES)), [VMEM] * 6, scratch=work)(*local_parts)
    heat = call(
        field_kernel,
        f32(TY, 3 + span // LANES, TX, LANES),
        [VMEM] * 11,
        scratch=work + [pltpu.VMEM(power, F32), pltpu.VMEM((CX, LANES), F32)],
    )(*local_parts, from_low, from_high, base, *inner)
    heat = lax.all_to_all(heat, "gz", split_axis=0, concat_axis=0, tiled=True)
    t, beside, first, last = call(first_kernel, (pencil, pencil, line, line), [VMEM] * 2)(base, heat)
    ends = [(i, i + 1) for i in range(n_z - 1, n_y * n_z - 1, n_z)]
    outer = lax.ppermute(t, ("gy", "gz"), ends + [(j, i) for i, j in ends])
    before = lax.ppermute(last, "gx", shifts(n_x, 1))
    after = lax.ppermute(first, "gx", shifts(n_x, -1))
    density = call(dense_kernel, tall, [VMEM] * 2)(packed, t)
    result = call(second_kernel, tall, [VMEM] * 7)(t, packed, heat, beside, outer, before, after)
    return result, density


def solution(mesh):
    return jax.shard_map(
        local,
        mesh=mesh,
        in_specs=(
            P(None, "gx", "gy", "gz"),
            P(None, "gx", "gy", "gz"),
            P("gx", "gy", "gz"),
            P(("gx", "gy", "gz"), None),
            P("gx", ("gy", "gz"), None),
            P("gx", ("gy", "gz"), None),
        ),
        out_specs=(P("gx", ("gy", "gz"), None), P("gx", ("gy", "gz"), None)),
        check_vma=False,
    )
```
